256 devices in a mesh: seq: 64 (over z, x_lo, y), dp: 4 (over x_hi, core).
Axes of the slice: x: 4 (x_hi: 2, x_lo: 2; x = x_hi * 2 + x_lo), y: 4, z: 8, core: 2. Of those that a mesh axis runs over, the one named last changes fastest.
Arguments:
- tokens: bfloat16 [4, 128, 256, 1152], P('dp', 'seq'), may hold values from -500 to 500
- d_out: bfloat16 [4, 128, 256, 1152], P('dp', 'seq'), may hold values from -6 to 6
- modulation: float32 [4, 8, 3, 1152], P('dp'), may hold values from -10 to 10
- w_qkv: bfloat16 [1728, 1152], P('dp'), may hold values from -1 to 1
- w_out: bfloat16 [1152, 576], P('dp'), may hold values from -0.25 to 0.25
Outputs:
- d_tokens: bfloat16 [4, 128, 256, 1152], P('dp', 'seq')
- d_modulation: float32 [4, 8, 3, 1152], P('dp')
- g_qkv: float32 [1728, 1152], P('dp', 'seq')
- g_out: float32 [1152, 576], P('dp', 'seq')
The draws below stay inside these ranges and needn't reach their ends.
All inputs are finite; a program needn't handle non-finite values.
Results may differ from the reference program's by a relative error of at most 0.0065.
The reference program's roundings to bfloat16 on the way count: a program that leaves them out, or rounds other values in their place, can miss the bound.
Values may be sent and summed in bfloat16 or wider, within the bound.
A program may use at most 128 MiB of HBM per device.

```python
import math
from functools import partial
import jax
import jax.numpy as jnp
from jax import lax

D = 1152
HD = 72
HEADS = 8
FRAMES = 16
PATCHES = 256
GROUPS = 4
GF = 128
CLIPS_G = 8
HE = 576


def draw_tokens(key, part):
    key = jax.random.fold_in(key, 11)
    first, second, third = jax.random.split(key, 3)
    shape = (GROUPS, GF, PATCHES, D)
    channel = jnp.exp(jax.random.uniform(second, (D,), jnp.float32) * math.log(10.0))
    rowwise = jnp.exp(jax.random.uniform(third, (GROUPS, GF, PATCHES, 1), jnp.float32) * math.log(10.0))
    base = jax.random.truncated_normal(first, -4.0, 4.0, shape, jnp.float32)
    return (base * channel * rowwise).astype(jnp.bfloat16)


def draw_modulation(key, part):
    key = jax.random.fold_in(key, 12)
    first = jax.random.fold_in(key, 0)
    third = jax.random.fold_in(key, 2)
    fourth = jax.random.fold_in(key, 3)
    shape = (GROUPS, CLIPS_G, D)
    shift = 0.5 * jax.random.truncated_normal(first, -4.0, 4.0, shape, jnp.float32)
    scale = 0.3 * jax.random.truncated_normal(third, -4.0, 4.0, shape, jnp.float32)
    gate = jax.random.truncated_normal(fourth, -4.0, 4.0, shape, jnp.float32)
    return jnp.stack([shift, scale, gate], 2).astype(jnp.float32)


def draw_w_qkv(key, part):
    key = jax.random.fold_in(key, 13)
    first = jax.random.fold_in(key, 0)
    shape = (3, HEADS, HD, D)
    base = jax.random.truncated_normal(first, -4.0, 4.0, shape, jnp.float32)
    return (base.reshape(3 * HEADS * HD, D) / math.sqrt(D)).astype(jnp.bfloat16)


def level_of(own_key, shape, cuts, smallest, top_value):
    factor_of = 1.0
    for axis_at, blocks in cuts:
        heights = jax.random.uniform(jax.random.fold_in(jax.random.fold_in(own_key, 6), axis_at), (blocks,), jnp.float32, smallest / len(cuts), top_value / len(cuts))
        factor_of = factor_of * jnp.repeat(jnp.exp(heights), shape[axis_at] // blocks).reshape((-1,) + (1,) * (len(shape) - 1 - axis_at))
    return factor_of


def centred(key, extent, width, reach, pieces=(), held_as=jnp.bfloat16):
    drawn = width * jax.random.normal(key, extent, jnp.float32)
    if pieces:
        drawn = drawn * level_of(key, extent, pieces, -0.22, 0.18)
    return jnp.clip(drawn, -reach, reach).astype(held_as)


def setup_inputs(seed: int = 0) -> dict:
    streams_of = jax.random.split(jax.random.key(seed), 6)
    tokens = draw_tokens(jax.random.fold_in(streams_of[5], 71), 0)
    d_out = centred(streams_of[1], (GROUPS, GF, PATCHES, D), 1.0, 6.0, ((0, 4), (1, 64)))
    modulation = draw_modulation(jax.random.fold_in(streams_of[5], 71), 0)
    w_qkv = draw_w_qkv(jax.random.fold_in(streams_of[5], 71), 0)
    w_out = centred(streams_of[4], (D, HE), HE ** -0.5, 0.25, ((0, 4),))
    return {"tokens": tokens, "d_out": d_out, "modulation": modulation, "w_qkv": w_qkv, "w_out": w_out}


EPS = 1e-06

def chopped(value):
    return lax.optimization_barrier(value.astype(jnp.bfloat16)).astype(jnp.float32)

def clip_pass(carry, item, w_qkv, w_out):
    acc_qkv, acc_out = carry
    block, grad_in, mod = item
    shift, scale, gate = (mod[0], mod[1], mod[2])
    inv = 1.0 / math.sqrt(HD)
    xf = block.astype(jnp.float32).reshape(-1, D)
    center = xf - lax.optimization_barrier(jnp.mean(xf, -1, keepdims=True))
    var = lax.optimization_barrier(jnp.mean(center * center, -1, keepdims=True))
    rstd = lax.rsqrt(var + EPS)
    normed = center * rstd
    modulated = (normed * (1.0 + scale) + shift).astype(jnp.bfloat16)
    qkv = jnp.dot(modulated, w_qkv.T, preferred_element_type=jnp.float32)
    qkv = chopped(qkv).reshape(FRAMES, -1, 3, HEADS, HD)
    query, keys, values = (qkv[:, :, 0], qkv[:, :, 1], qkv[:, :, 2])
    scores = jnp.einsum('fphe,gphe->phfg', query, keys) * inv
    probs = jax.nn.softmax(scores, axis=-1)
    probs_b = chopped(probs)
    attended = jnp.einsum('phfg,gphe->fphe', probs_b, values).astype(jnp.bfloat16).reshape(-1, HEADS * HD)
    branch = jnp.dot(attended, w_out.T, preferred_element_type=jnp.float32)
    dyf = grad_in.astype(jnp.float32).reshape(-1, D)
    d_gate = lax.optimization_barrier(jnp.sum(dyf * branch, 0))
    d_branch = (gate * dyf).astype(jnp.bfloat16)
    acc_out = acc_out + jnp.dot(d_branch.T, attended, preferred_element_type=jnp.float32)
    d_att = chopped(jnp.dot(d_branch, w_out, preferred_element_type=jnp.float32)).reshape(FRAMES, -1, HEADS, HD)
    d_probs = jnp.einsum('fphe,gphe->phfg', d_att, values)
    d_values = jnp.einsum('phfg,fphe->gphe', probs_b, d_att)
    d_scores = probs * (d_probs - lax.optimization_barrier(jnp.sum(probs * d_probs, -1, keepdims=True))) * inv
    d_scores = chopped(d_scores)
    d_query = jnp.einsum('phfg,gphe->fphe', d_scores, keys)
    d_keys = jnp.einsum('phfg,fphe->gphe', d_scores, query)
    d_qkv = jnp.stack([d_query, d_keys, d_values], 2).astype(jnp.bfloat16).reshape(-1, 3 * HEADS * HD)
    acc_qkv = acc_qkv + jnp.dot(d_qkv.T, modulated, preferred_element_type=jnp.float32)
    d_mod_in = chopped(jnp.dot(d_qkv, w_qkv, preferred_element_type=jnp.float32))
    d_shift = lax.optimization_barrier(jnp.sum(d_mod_in, 0))
    d_scale = lax.optimization_barrier(jnp.sum(d_mod_in * normed, 0))
    d_normed = d_mod_in * (1.0 + scale)
    mean_one = lax.optimization_barrier(jnp.mean(d_normed, -1, keepdims=True))
    mean_two = lax.optimization_barrier(jnp.mean(d_normed * normed, -1, keepdims=True))
    d_in = dyf + rstd * (d_normed - mean_one - normed * mean_two)
    result = d_in.astype(jnp.bfloat16).reshape(FRAMES, -1, D)
    return ((acc_qkv, acc_out), (result, jnp.stack([d_shift, d_scale, d_gate], 0)))

def reference(tokens, d_out, modulation, w_qkv, w_out):
    blocks = tokens.reshape(-1, FRAMES, tokens.shape[2], D)
    grads = d_out.reshape(-1, FRAMES, tokens.shape[2], D)
    mods = modulation.reshape(-1, 3, D)
    start = (jnp.zeros((3 * HEADS * HD, D), jnp.float32), jnp.zeros((D, HEADS * HD), jnp.float32))
    step = partial(clip_pass, w_qkv=w_qkv, w_out=w_out)
    (g_qkv, g_out), (d_in, d_mod) = lax.scan(step, start, (blocks, grads, mods))
    return (d_in.reshape(tokens.shape), d_mod.reshape(modulation.shape), g_qkv, g_out)
```

```python
import functools
import math

import jax
import jax.numpy as jnp
from jax import lax
from jax.experimental import pallas as pl
from jax.experimental.pallas import tpu as pltpu
from jax.sharding import PartitionSpec as P

MESH = pl.DeviceIdType.MESH
F32 = jnp.float32
BF16 = jnp.bfloat16

WIDTH = 1152
HEADS = 8
HD = 72
FRAMES = 16
CLIP_DEVICES = 8
CHUNKS = 4
CHUNK = 128
ROWS = 512
SHARD_Q = 432
SHARD_O = 288
HALF_Q = 896
HALF_O = 640
START_O = 512
SLOT_E = 80
EPS = 1e-06
VMEM_BYTES = 56 * 1024 * 1024
NEG = -1e30

PIECES = ((0, 0, 512), (0, 512, 384), (1, 0, 256), (1, 256, 384))
FIRST_PIECES = ((0, 2), (1, 3))
BLOCK_Q = 144
BLOCK_O = SLOT_E
OFFSETS = (4, 3, 5, 2, 6, 1, 7, 0)
STEPS = 4


def dot(left, right, contract):
    return lax.dot_general(
        left, right, ((contract[:1], contract[1:]), ((), ())), preferred_element_type=F32
    )


def place():
    seq, dp = lax.axis_index("seq"), lax.axis_index("dp")
    clip, spot = lax.div(seq, 8), lax.rem(seq, 8)
    half, core = lax.div(dp, 2), lax.rem(dp, 2)
    return seq, dp, clip, spot, half, core


def column(part, head):
    block = part * HEADS + head
    return block * HD if block < 12 else HALF_Q + (block - 12) * HD


def normalise(x):
    center = x - jnp.mean(x, -1, keepdims=True)
    var = jnp.mean(center * center, -1, keepdims=True)
    rstd = lax.rsqrt(var + EPS)
    return center * rstd, rstd


def signal_all(barrier, devices):
    for device in devices:
        pl.semaphore_signal(barrier, inc=1, device_id=device, device_id_type=MESH)


def wait_bytes(ref, sem):
    pltpu.make_async_copy(ref, ref, sem).wait()


def spread_kernel(
    tok, dout, mod, wq, wo, m_all, d_all, wq_all, wo_all,
    m_send, d_send, a_send, a_recv, w_send, w_recv, here,
):
    seq, dp, clip, spot, half, core = place()
    twin = {"seq": seq, "dp": half * 2 + 1 - core}
    across = {
        "seq": clip * 8 + (1 - lax.div(spot, 4)) * 4 + lax.rem(spot, 4),
        "dp": (1 - half) * 2 + core,
    }

    def peer(d):
        return {"seq": clip * 8 + lax.rem(spot + d, 8), "dp": dp}

    barrier = pltpu.get_barrier_semaphore()
    signal_all(barrier, [peer(d) for d in range(1, 8)] + [twin, across])
    pl.semaphore_wait(barrier, 9)

    def rows(h, c):
        return (
            wq_all.at[pl.ds(pl.multiple_of(h * HALF_Q + c * SHARD_Q, 16), SHARD_Q)],
            wo_all.at[pl.ds(pl.multiple_of((h * 2 + c) * SHARD_O, 16), SHARD_O)],
        )

    def push(src, dst, at, device):
        copies = [
            pltpu.make_async_remote_copy(
                src_ref=src[i], dst_ref=dst[i], send_sem=w_send.at[at + i],
                recv_sem=w_recv.at[at + i], device_id=device, device_id_type=MESH,
            )
            for i in range(2)
        ]
        for copy in copies:
            copy.start()
        return copies

    own = rows(half, core)
    sent = push((wq, wo), own, 2, across)
    sent += push((wq, wo), own, 0, twin)
    locals_ = [pltpu.make_async_copy(src, own[i], here.at[i]) for i, src in enumerate((wq, wo))]
    for copy in locals_:
        copy.start()
    zeros = jnp.zeros((HALF_Q - 2 * SHARD_Q, WIDTH), BF16)
    wq_all[2 * SHARD_Q:HALF_Q, :] = zeros
    wq_all[HALF_Q + 2 * SHARD_Q:, :] = zeros

    own_mod = mod[0, pl.ds(clip, 1)].reshape(3, WIDTH)
    shift, scale = own_mod[0:1], 1.0 + own_mod[1:2]

    def arranged(x):
        return jnp.concatenate(
            [x[f, 8 * g:8 * g + 8] for g in range(CHUNKS) for f in range(2)], 0
        ).astype(BF16).reshape(CHUNKS, 16, WIDTH)

    def blocks(d):
        first = pl.multiple_of(lax.rem(spot + d, 8) * 32, 32)
        x = tok[0, :, pl.ds(first, 32), :].astype(F32)
        g = dout[0, :, pl.ds(first, 32), :].astype(F32)
        normed, _ = normalise(x)
        return arranged(normed * scale + shift), arranged(g)

    mine = pl.ds(pl.multiple_of(spot * 16, 16), 16)

    def copies(d):
        return [
            pltpu.make_async_remote_copy(
                src_ref=src.at[d], dst_ref=dst.at[:, mine, :], send_sem=a_send.at[i, d],
                recv_sem=a_recv.at[i, d], device_id=peer(d), device_id_type=MESH,
            )
            for i, (src, dst) in enumerate(((m_send, m_all), (d_send, d_all)))
        ]

    @pl.loop(1, 8)
    def _(d):
        m_send[d], d_send[d] = blocks(d)
        for copy in copies(d):
            copy.start()

    m_all[:, mine, :], d_all[:, mine, :] = blocks(0)
    other = rows(1 - half, core)
    for i in range(2):
        wait_bytes(other[i], w_recv.at[2 + i])
    sent += push(other, other, 4, twin)
    last = rows(1 - half, 1 - core)
    for i, ref in enumerate(rows(half, 1 - core)):
        wait_bytes(ref, w_recv.at[i])
    for d in range(1, 8):
        for copy in copies(d):
            copy.wait_recv()
    for i, ref in enumerate(last):
        wait_bytes(ref, w_recv.at[4 + i])
    for d in range(1, 8):
        for copy in copies(d):
            copy.wait_send()
    for copy in sent:
        copy.wait_send()
    for copy in locals_:
        copy.wait()


def middle_kernel(
    m_all, d_all, wq_all, wo_all, mod, d_in, gq, go, gate_part,
    qkv, datt, att, att_slots, dbranch, dqkv, turned,
):
    _, _, clip, _, _, _ = place()
    gate = mod[0, pl.ds(clip, 1)].reshape(3, WIDTH)[2:3]
    inv = 1.0 / math.sqrt(HD)

    m = m_all[...].reshape(ROWS, WIDTH)

    @pl.loop(0, 7)
    def _(n):
        at = pl.ds(pl.multiple_of(n * 256, 256), 256)
        qkv[:, at] = dot(m, wq_all[at, :], (1, 1)).astype(BF16)

    @pl.loop(0, CHUNKS)
    def _(c):
        at = pl.ds(pl.multiple_of(c * CHUNK, CHUNK), CHUNK)
        dbranch[at, :] = (gate * d_all[c].astype(F32)).astype(BF16)

    datt[...] = dot(dbranch[...], wo_all[...], (1, 0)).astype(BF16)

    for ref, start in ((dqkv, 2 * SHARD_Q), (dqkv, HALF_Q + 2 * SHARD_Q)):
        ref[:, start:start + 32] = jnp.zeros((ROWS, 32), BF16)
    att_slots[...] = jnp.zeros_like(att_slots)

    same = lax.rem(lax.broadcasted_iota(jnp.int32, (CHUNK, CHUNK), 0), 8) == lax.rem(
        lax.broadcasted_iota(jnp.int32, (CHUNK, CHUNK), 1), 8
    )

    @pl.loop(0, CHUNKS)
    def _(c):
        at = pl.ds(pl.multiple_of(c * CHUNK, CHUNK), CHUNK)
        for h in range(HEADS):
            cq, ck, cv = (column(part, h) for part in range(3))
            q, k, v = (qkv[at, col:col + HD] for col in (cq, ck, cv))
            da = datt[at, h * HD:h * HD + HD]
            scores = jnp.where(same, dot(q, k, (1, 1)) * inv, NEG)
            e = jnp.exp(scores - jnp.max(scores, -1, keepdims=True))
            probs = e / jnp.sum(e, -1, keepdims=True)
            probs_b = probs.astype(BF16)
            attended = dot(probs_b, v, (1, 0)).astype(BF16)
            att[at, h * HD:h * HD + HD] = attended
            att_slots[at, h * SLOT_E:h * SLOT_E + HD] = attended
            d_probs = dot(da, v, (1, 1))
            spread = jnp.sum(probs * d_probs, -1, keepdims=True)
            d_scores = (probs * (d_probs - spread) * inv).astype(BF16)
            dqkv[at, cq:cq + HD] = dot(d_scores, k, (1, 0)).astype(BF16)
            dqkv[at, ck:ck + HD] = dot(d_scores, q, (0, 0)).astype(BF16)
            dqkv[at, cv:cv + HD] = dot(probs_b, da, (0, 0)).astype(BF16)

    for n in range(3):
        at = slice(n * 384, n * 384 + 384)
        part = dot(dqkv[...], wq_all[:, at], (1, 0)).astype(BF16)
        d_in[:, :, at] = part.reshape(CHUNKS, CHUNK, 384)

    turned[...] = m.T
    for h in range(2):
        @pl.loop(0, 7)
        def _(n):
            at = pl.ds(pl.multiple_of(n * 128, 128), 128)
            src = pl.ds(pl.multiple_of(h * HALF_Q + n * 128, 128), 128)
            gq[h, :, at] = dot(turned[...], dqkv[:, src], (1, 0)).astype(BF16)

    slots = att_slots[...].T
    for h in range(2):
        go[h] = dot(slots, dbranch[:, h * START_O:h * START_O + HALF_O], (1, 0)).astype(BF16)

    for n in range(3):
        at = slice(n * 384, n * 384 + 384)
        branch = dot(att[...], wo_all[at, :], (1, 1))
        grads = d_all[:, :, at].reshape(ROWS, 384).astype(F32)
        gate_part[:, at] = jnp.sum(branch * grads, 0, keepdims=True)


def finish_kernel(
    d_in, gq, go, gate_part, tok, dout, mod, d_tok, d_mod, oq, oo,
    back, xq, xo, sq, so, rq, ro, stage, final, part, parts,
    b_send, b_recv, x_send, x_recv, c_send, c_recv, p_send, p_recv,
    z_send, z_recv, f_send, f_recv,
):
    seq, dp, clip, spot, half, core = place()
    twin = {"seq": seq, "dp": half * 2 + 1 - core}

    def peer(d):
        return {"seq": clip * 8 + lax.rem(spot + d, 8), "dp": dp}

    def along(d):
        return {"seq": lax.rem(clip + d, 8) * 8 + spot, "dp": dp}

    def owner(d, low):
        return {"seq": clip * 8 + lax.rem(spot + d, 8), "dp": core * 2 + low}

    def source(d, h):
        return {"seq": clip * 8 + lax.rem(spot + 8 - d, 8), "dp": h * 2 + half}

    barrier = pltpu.get_barrier_semaphore()
    signal_all(barrier, [twin] + [peer(d) for d in range(1, 8)] + [along(d) for d in range(1, 8)])
    signal_all(barrier, [source(d, h) for d in range(1, 8) for h in range(2)])
    for h in range(2):
        @pl.when(jnp.logical_or(half != core, h != half))
        def _():
            signal_all(barrier, [source(0, h)])
    pl.semaphore_wait(barrier, jnp.where(half == core, 30, 31))

    def back_copy(d):
        to = pl.ds(pl.multiple_of(lax.rem(spot + d, 8) * 16, 16), 16)
        return pltpu.make_async_remote_copy(
            src_ref=d_in.at[:, to, :], dst_ref=back.at[d], send_sem=b_send.at[d],
            recv_sem=b_recv.at[d], device_id=peer(d), device_id_type=MESH,
        )

    for d in range(1, 8):
        back_copy(d).start()

    def block(ref, z):
        size = BLOCK_Q if ref is xq or ref is gq else BLOCK_O
        return pl.ds(pl.multiple_of(z * size, 16), size)

    def pair_copies(i):
        z = lax.rem(clip + OFFSETS[i], 8)
        return [
            pltpu.make_async_remote_copy(
                src_ref=src.at[1 - core, block(dst, z), :], dst_ref=dst.at[block(dst, z), :],
                send_sem=x_send.at[i, n], recv_sem=x_recv.at[i, n],
                device_id=twin, device_id_type=MESH,
            )
            for n, (src, dst) in enumerate(((gq, xq), (go, xo)))
        ]

    for i in range(8):
        for copy in pair_copies(i):
            copy.start()

    def own(which, z, first, lanes):
        src, dst = (gq, xq) if which == 0 else (go, xo)
        at = block(dst, z)
        return src[core, at, first:first + lanes].astype(F32) + dst[at, first:first + lanes].astype(F32)

    def pieces(k, way):
        return FIRST_PIECES[way] if k == 0 else range(len(PIECES))

    def chain_copy(way, k, n):
        which, first, lanes = PIECES[n]
        src, dst = (sq, rq) if which == 0 else (so, ro)
        return pltpu.make_async_remote_copy(
            src_ref=src.at[way, k, :, first:first + lanes],
            dst_ref=dst.at[way, k, :, first:first + lanes],
            send_sem=c_send.at[way, k, n], recv_sem=c_recv.at[way, k, n],
            device_id=along(1 if way == 0 else 7), device_id_type=MESH,
        )

    def arrived(way, k, n):
        which, first, lanes = PIECES[n]
        chain_copy(way, k, n).wait_recv()
        return (rq, ro)[which][way, k, :, first:first + lanes].astype(F32)

    def chain_step(k):
        for way in range(2):
            for copy in pair_copies(0 if k == 0 else 2 * k - 1 + way) if not (k == 0 and way) else []:
                copy.wait_recv()
        for n in range(len(PIECES)):
            for way in range(2):
                if n not in pieces(k, way):
                    continue
                which, first, lanes = PIECES[n]
                z = lax.rem(clip + (4 - k if way == 0 else 4 + k), 8)
                total = own(which, z, first, lanes)
                if k and n in pieces(k - 1, way):
                    total = total + arrived(way, k - 1, n)
                (sq, so)[which][way, k, :, first:first + lanes] = total.astype(BF16)
                chain_copy(way, k, n).start()

    chain_step(0)

    mod_here = mod[0, pl.ds(clip, 1)].reshape(3, WIDTH)
    scale = 1.0 + mod_here[1:2]
    mine = pl.ds(pl.multiple_of(spot * 16, 16), 16)

    def tokens_back(d, carry):
        b = back[d].astype(F32).reshape(64, WIDTH)
        b = jnp.stack(
            [
                jnp.concatenate([b[16 * g + 8 * f:16 * g + 8 * f + 8] for g in range(CHUNKS)], 0)
                for f in range(2)
            ],
            0,
        )
        rows = pl.ds(pl.multiple_of(lax.rem(spot + 8 - d, 8) * 32, 32), 32)
        normed, rstd = normalise(tok[0, :, rows, :].astype(F32))
        d_normed = b * scale
        one = jnp.mean(d_normed, -1, keepdims=True)
        two = jnp.mean(d_normed * normed, -1, keepdims=True)
        out = dout[0, :, rows, :].astype(F32) + rstd * (d_normed - one - normed * two)
        d_tok[0, :, rows, :] = out.astype(BF16)
        return (
            carry[0] + jnp.sum(b.reshape(8, 8, WIDTH), 0),
            carry[1] + jnp.sum((b * normed).reshape(8, 8, WIDTH), 0),
        )

    zero = jnp.zeros((8, WIDTH), F32)
    back[0] = d_in[:, mine, :]
    sums = tokens_back(0, (zero, zero))
    chain_step(1)
    for d in range(1, 8):
        back_copy(d).wait_recv()
    sums = lax.fori_loop(1, 8, tokens_back, sums)
    part[0:1] = jnp.sum(sums[0], 0, keepdims=True)
    part[1:2] = jnp.sum(sums[1], 0, keepdims=True)
    part[2:3] = gate_part[...]
    part[3:] = jnp.zeros((5, WIDTH), F32)

    def part_copy(d):
        return pltpu.make_async_remote_copy(
            src_ref=part, dst_ref=parts.at[d], send_sem=p_send.at[d],
            recv_sem=p_recv.at[d], device_id=peer(d), device_id_type=MESH,
        )

    for d in range(1, 8):
        part_copy(d).start()
    chain_step(2)
    total = part[...]
    for d in range(1, 8):
        part_copy(d).wait_recv()
        total = total + parts[d]
    d_mod[0, pl.ds(clip, 1)] = total[0:3].reshape(1, 3, WIDTH)

    def mod_copy(d):
        return pltpu.make_async_remote_copy(
            src_ref=d_mod.at[0, clip], dst_ref=d_mod.at[0, clip], send_sem=z_send.at[d],
            recv_sem=z_recv.at[d], device_id=along(d), device_id_type=MESH,
        )

    for d in range(1, 8):
        mod_copy(d).start()
    chain_step(3)
    for copy in pair_copies(7):
        copy.wait_recv()
    sums_ = []
    for which in range(2):
        whole = []
        for n, (which_n, first, lanes) in enumerate(PIECES):
            if which_n == which:
                total = own(which, clip, first, lanes)
                for way in range(2):
                    total = total + arrived(way, 3, n)
                whole.append(total.astype(BF16))
        sums_.append(jnp.concatenate(whole, 1))

    def widen(x, size, slot):
        count = 8 * slot
        row = lax.broadcasted_iota(jnp.int32, (count, x.shape[0]), 0)
        col = lax.broadcasted_iota(jnp.int32, (count, x.shape[0]), 1)
        inside = lax.rem(row, slot)
        pick = jnp.logical_and(col == lax.div(row, slot) * size + inside, inside < size)
        return dot(pick.astype(F32).astype(BF16), x, (1, 0)).astype(BF16)

    wide_q, wide_o = widen(sums_[0], 18, 32), widen(sums_[1], 9, 16)
    for j in range(8):
        for low in range(2):
            stage[j, low, 0:32, :] = wide_q[32 * j:32 * j + 32, 384 * low:384 * low + 512]
            stage[j, low, 32:48, 0:384] = wide_o[16 * j:16 * j + 16, 256 * low:256 * low + 384]
            stage[j, low, 32:48, 384:512] = jnp.zeros((16, 128), BF16)

    def owner_copy(d, low):
        to = half * 8 + d
        return pltpu.make_async_remote_copy(
            src_ref=stage.at[lax.rem(spot + d, 8), low], dst_ref=final.at[to],
            send_sem=f_send.at[d, low], recv_sem=f_recv.at[to],
            device_id=owner(d, low), device_id_type=MESH,
        )

    for d in range(1, 8):
        for low in range(2):
            owner_copy(d, low).start()
    for low in range(2):
        is_self = jnp.logical_and(core == half, core == low)

        @pl.when(is_self)
        def _():
            pltpu.make_async_copy(stage.at[spot, low], final.at[half * 8], f_recv.at[half * 8]).start()

        @pl.when(jnp.logical_not(is_self))
        def _():
            owner_copy(0, low).start()

    for i in range(16):
        wait_bytes(final.at[i], f_recv.at[i])
    total = final[0].astype(F32)
    for i in range(1, 16):
        total = total + final[i].astype(F32)
    got_q = jnp.where(core == 0, total[0:32, 0:SHARD_Q], total[0:32, 48:48 + SHARD_Q])
    first_o = 64 * half + 32 * core
    got_o = total[32:48, 0:SHARD_O]
    for start in (32, 64, 96):
        got_o = jnp.where(first_o == start, total[32:48, start:start + SHARD_O], got_o)
    got_q = jnp.concatenate([jnp.concatenate([got_q, jnp.zeros((32, 80), F32)], 1), jnp.zeros((96, 512), F32)], 0)
    got_o = jnp.concatenate([jnp.concatenate([got_o, jnp.zeros((16, 96), F32)], 1), jnp.zeros((112, 384), F32)], 0)
    oq[...] = got_q.T[0:SHARD_Q, 0:18]
    oo[...] = got_o.T[0:SHARD_O, 0:9]

    for d in range(1, 8):
        mod_copy(d).wait()
        back_copy(d).wait_send()
        part_copy(d).wait_send()
        for low in range(2):
            owner_copy(d, low).wait_send()
    for low in range(2):
        @pl.when(jnp.logical_or(core != half, core != low))
        def _():
            owner_copy(0, low).wait_send()
    for i in range(8):
        for copy in pair_copies(i):
            copy.wait_send()
    for k in range(STEPS):
        for way in range(2):
            for n in pieces(k, way):
                chain_copy(way, k, n).wait_send()


def call(kernel, outs, scratch, count, collective_id=None):
    params = dict(vmem_limit_bytes=VMEM_BYTES)
    if collective_id is not None:
        params.update(collective_id=collective_id, has_side_effects=True)
    whole = pl.BlockSpec(memory_space=pltpu.VMEM)
    return pl.pallas_call(
        kernel,
        out_shape=[jax.ShapeDtypeStruct(shape, dtype) for shape, dtype in outs],
        in_specs=[whole] * count,
        out_specs=[whole] * len(outs),
        scratch_shapes=scratch,
        compiler_params=pltpu.CompilerParams(**params),
    )


def body(tokens, d_out, modulation, w_qkv, w_out):
    dma = pltpu.SemaphoreType.DMA
    vmem = pltpu.VMEM
    moved = (CHUNKS, CHUNK, WIDTH)
    m_all, d_all, wq_all, wo_all = call(
        spread_kernel,
        [(moved, BF16), (moved, BF16), ((2 * HALF_Q, WIDTH), BF16), ((WIDTH, HEADS * HD), BF16)],
        [
            vmem((8, CHUNKS, 16, WIDTH), BF16), vmem((8, CHUNKS, 16, WIDTH), BF16),
            dma((2, 8)), dma((2, 8)), dma((6,)), dma((6,)), dma((2,)),
        ],
        5, 0,
    )(tokens, d_out, modulation, w_qkv, w_out)
    d_in, gq, go, gate_part = call(
        middle_kernel,
        [
            (moved, BF16), ((2, WIDTH, HALF_Q), BF16),
            ((2, HEADS * SLOT_E, HALF_O), BF16), ((1, WIDTH), F32),
        ],
        [
            vmem((ROWS, 2 * HALF_Q), BF16), vmem((ROWS, HEADS * HD), BF16),
            vmem((ROWS, HEADS * HD), BF16), vmem((ROWS, HEADS * SLOT_E), BF16),
            vmem((ROWS, WIDTH), BF16), vmem((ROWS, 2 * HALF_Q), BF16), vmem((WIDTH, ROWS), BF16),
        ],
        5,
    )(m_all, d_all, wq_all, wo_all, modulation)
    return call(
        finish_kernel,
        [
            (tokens.shape, BF16), (modulation.shape, F32),
            ((SHARD_Q, 18), F32), ((SHARD_O, 9), F32),
        ],
        [
            vmem((8, CHUNKS, 16, WIDTH), BF16),
            vmem((WIDTH, HALF_Q), BF16), vmem((HEADS * SLOT_E, HALF_O), BF16),
            vmem((2, STEPS, BLOCK_Q, HALF_Q), BF16), vmem((2, STEPS, BLOCK_O, HALF_O), BF16),
            vmem((2, STEPS, BLOCK_Q, HALF_Q), BF16), vmem((2, STEPS, BLOCK_O, HALF_O), BF16),
            vmem((8, 2, 48, 512), BF16), vmem((16, 48, 512), BF16),
            vmem((8, WIDTH), F32), vmem((8, 8, WIDTH), F32),
            dma((8,)), dma((8,)), dma((8, 2)), dma((8, 2)),
            dma((2, STEPS, len(PIECES))), dma((2, STEPS, len(PIECES))),
            dma((8,)), dma((8,)), dma((8,)), dma((8,)), dma((8, 2)), dma((16,)),
        ],
        7, 1,
    )(d_in, gq, go, gate_part, tokens, d_out, modulation)


def solution(mesh):
    in_specs = (
        P("dp", "seq", None, None),
        P("dp", "seq", None, None),
        P("dp", None, None, None),
        P("dp", None),
        P("dp", None),
    )
    out_specs = (
        P("dp", "seq", None, None),
        P("dp", None, None, None),
        P("dp", "seq"),
        P("dp", "seq"),
    )
    return jax.shard_map(body, mesh=mesh, in_specs=in_specs, out_specs=out_specs, check_vma=False)
```

```python
import math

import jax
import jax.numpy as jnp
from jax import lax
from jax.experimental import pallas as pl
from jax.experimental.pallas import tpu as pltpu
from jax.sharding import PartitionSpec as P

MESH = pl.DeviceIdType.MESH
F32 = jnp.float32
BF16 = jnp.bfloat16

WIDTH = 1152
HEADS = 8
HD = 72
FRAMES = 16
CLIP_DEVICES = 8
CHUNKS = 4
CHUNK = 128
ROWS = 512
SHARD_Q = 432
SHARD_O = 288
HALF_Q = 896
HALF_O = 640
START_O = 512
SLOT_E = 80
EPS = 1e-06
VMEM_BYTES = 56 * 1024 * 1024

PIECES = ((0, 0, 512), (0, 512, 384), (1, 0, 256), (1, 256, 384))
FIRST_PIECES = ((0, 2), (1, 3))
BLOCK_Q = 144
BLOCK_O = SLOT_E
OFFSETS = (4, 3, 5, 2, 6, 1, 7, 0)
STEPS = 4
HALF_ROWS = 256

PIECES_WQ = (((0, 64), (64, 48), (112, 64), (176, 48)), ((224, 64), (288, 48), (336, 48), (384, 48)))
PIECES_WO = (((0, 48), (48, 32), (80, 32), (112, 32)), ((144, 48), (192, 32), (224, 32), (256, 32)))


def dot(left, right, contract):
    return lax.dot_general(
        left, right, ((contract[:1], contract[1:]), ((), ())), preferred_element_type=F32
    )


def place():
    seq, dp = lax.axis_index("seq"), lax.axis_index("dp")
    clip, spot = lax.div(seq, 8), lax.rem(seq, 8)
    half, core = lax.div(dp, 2), lax.rem(dp, 2)
    return seq, dp, clip, spot, half, core


def column(part, head):
    block = part * HEADS + head
    return block * HD if block < 12 else HALF_Q + (block - 12) * HD


def normalise(x):
    center = x - jnp.mean(x, -1, keepdims=True)
    var = jnp.mean(center * center, -1, keepdims=True)
    rstd = lax.rsqrt(var + EPS)
    return center * rstd, rstd


def signal_all(barrier, devices):
    for device in devices:
        pl.semaphore_signal(barrier, inc=1, device_id=device, device_id_type=MESH)


def by_parity(clip, act):
    for parity in range(2):
        @pl.when(lax.rem(clip, 2) == parity)
        def _():
            act(parity)


def wait_bytes(ref, sem):
    pltpu.make_async_copy(ref, ref, sem).wait()


def fused_kernel(
    tok_in, dout_in, mod, wq, wo, tok_out, d_mod, oq, oo,
    tok, dout, m_send, d_send, m_all, d_all, wq_all, wo_all,
    qkv, datt, att, att_slots, dbranch, dqkv, turned, d_in, gq, go,
    back, xq, xo, sq, so, rq, ro, stage, final, part, parts, mods,
    here, a_send, a_recv, own_send, own_recv, w_send, w_recv, v_send, v_recv, t_send, t_recv,
    b_send, b_recv, x_send, x_recv, c_send, c_recv, p_send, p_recv,
    z_send, z_recv, f_send, f_recv,
):
    seq, dp, clip, spot, half, core = place()
    twin = {"seq": seq, "dp": half * 2 + 1 - core}
    across = {
        "seq": clip * 8 + (1 - lax.div(spot, 4)) * 4 + lax.rem(spot, 4),
        "dp": (1 - half) * 2 + core,
    }

    def peer(d):
        return {"seq": clip * 8 + lax.rem(spot + d, 8), "dp": dp}

    def along(d):
        return {"seq": lax.rem(clip + d, 8) * 8 + spot, "dp": dp}

    def owner(d, low):
        return {"seq": clip * 8 + lax.rem(spot + d, 8), "dp": core * 2 + low}

    def source(d, h):
        return {"seq": clip * 8 + lax.rem(spot + 8 - d, 8), "dp": h * 2 + half}

    def remote(src, dst, send, recv, device):
        return pltpu.make_async_remote_copy(
            src_ref=src, dst_ref=dst, send_sem=send, recv_sem=recv,
            device_id=device, device_id_type=MESH,
        )

    loads = [
        pltpu.make_async_copy(tok_in.at[0], tok, here.at[0]),
        pltpu.make_async_copy(dout_in.at[0], dout, here.at[1]),
    ]
    for copy in loads:
        copy.start()
    barrier = pltpu.get_barrier_semaphore()
    signal_all(barrier, [twin, across] + [peer(d) for d in range(1, 8)] + [along(d) for d in range(1, 8)])
    signal_all(barrier, [source(d, h) for d in range(1, 8) for h in range(2)])
    for h in range(2):
        @pl.when(jnp.logical_or(half != core, h != half))
        def _():
            signal_all(barrier, [source(0, h)])
    pl.semaphore_wait(barrier, jnp.where(half == core, 31, 32))

    shards, wholes = (wq, wo), (wq_all, wo_all)

    def first_row(n, h, c):
        return h * HALF_Q + c * SHARD_Q if n == 0 else (h * 2 + c) * SHARD_O

    def rows(n, h, c, at):
        return wholes[n].at[pl.ds(pl.multiple_of(first_row(n, h, c) + at[0], 16), at[1])]

    def entire(n):
        return (0, (SHARD_Q, SHARD_O)[n])

    def piece(n, parity, i):
        return (PIECES_WQ, PIECES_WO)[n][parity][i]

    def own_copy(n):
        return remote(shards[n], rows(n, half, core, entire(n)), own_send.at[n], own_recv.at[n], twin)

    def keep_copy(n):
        return pltpu.make_async_copy(shards[n], rows(n, half, core, entire(n)), here.at[2 + n])

    def across_copy(n, parity, i):
        at = piece(n, parity, i)
        return remote(
            shards[n].at[pl.ds(at[0], at[1])], rows(n, half, core, at),
            w_send.at[n, i], w_recv.at[n, i], across,
        )

    def passed(n, parity, i):
        return rows(n, 1 - half, core, piece(n, parity, i))

    def along_copy(n, parity, i):
        ref = passed(n, parity, i)
        return remote(ref, ref, v_send.at[n, i], v_recv.at[n, i], along(1 if i % 2 == 0 else 7))

    def twin_copy(n, parity, i, own):
        ref = passed(n, parity, i)
        return remote(ref, ref, t_send.at[n, i, own], t_recv.at[n, i, own], twin)

    def send_across(parity):
        for i in range(4):
            for n in range(2):
                across_copy(n, parity, i).start()

    by_parity(clip, send_across)
    for n in range(2):
        keep_copy(n).start()
        own_copy(n).start()
    zeros = jnp.zeros((HALF_Q - 2 * SHARD_Q, WIDTH), BF16)
    wq_all[2 * SHARD_Q:HALF_Q, :] = zeros
    wq_all[HALF_Q + 2 * SHARD_Q:, :] = zeros

    own_mod = mod[0, :, pl.ds(clip, 1), :].reshape(3, WIDTH)
    shift, scale, gate = own_mod[0:1], 1.0 + own_mod[1:2], own_mod[2:3]
    mine = pl.ds(pl.multiple_of(spot * 16, 16), 16)

    def arranged(x):
        return jnp.concatenate(
            [x[f, 8 * g:8 * g + 8] for g in range(2) for f in range(2)], 0
        ).astype(BF16).reshape(2, 16, WIDTH)

    def patches(part, j):
        return pl.ds(pl.multiple_of(j * 32 + part * 16, 16), 16)

    def blocks(part, d):
        at = patches(part, lax.rem(spot + d, 8))
        normed, _ = normalise(tok[:, at, :].astype(F32))
        return arranged(normed * scale + shift), arranged(dout[:, at, :].astype(F32))

    def spread_copies(part, d):
        return [
            remote(
                src.at[part, d], dst.at[2 * part:2 * part + 2, mine, :],
                a_send.at[i, part, d], a_recv.at[i, part, d], peer(d),
            )
            for i, (src, dst) in enumerate(((m_send, m_all), (d_send, d_all)))
        ]

    for copy in loads:
        copy.wait()
    for part_ in range(2):
        @pl.loop(1, 8)
        def _(d):
            m_send[part_, d], d_send[part_, d] = blocks(part_, d)
            for copy in spread_copies(part_, d):
                copy.start()

        at = slice(2 * part_, 2 * part_ + 2)
        m_all[at, mine, :], d_all[at, mine, :] = blocks(part_, 0)

    for ref, start in ((dqkv, 2 * SHARD_Q), (dqkv, HALF_Q + 2 * SHARD_Q)):
        ref[:, start:start + 32] = jnp.zeros((ROWS, 32), BF16)
    att_slots[...] = jnp.zeros_like(att_slots)

    for i in range(4):
        def hand_on(parity):
            for n in range(2):
                across_copy(n, parity, i).wait_recv()
                along_copy(n, parity, i).start()
                twin_copy(n, parity, i, 0).start()

        by_parity(clip, hand_on)
    for i in range(4):
        def hand_twin(parity):
            for n in range(2):
                along_copy(n, 1 - parity, i).wait_recv()
                twin_copy(n, 1 - parity, i, 1).start()

        by_parity(clip, hand_twin)
    for n in range(2):
        keep_copy(n).wait()
        own_copy(n).wait_recv()

    def from_twin(parity):
        for i in range(4):
            for n in range(2):
                twin_copy(n, parity, i, 0).wait_recv()
                twin_copy(n, 1 - parity, i, 1).wait_recv()

    by_parity(clip, from_twin)

    inv = 1.0 / math.sqrt(HD)
    kept = (
        lax.broadcasted_iota(jnp.int32, (1, 8, CHUNK), 1)
        == lax.rem(lax.broadcasted_iota(jnp.int32, (1, 8, CHUNK), 2), 8)
    ).astype(F32)

    def attention(at):
        cols = [[column(part, h) for part in range(3)] for h in range(HEADS)]
        q, k, v = (
            [qkv[at, cols[h][part]:cols[h][part] + HD] for h in range(HEADS)] for part in range(3)
        )
        da = [datt[at, h * HD:h * HD + HD] for h in range(HEADS)]
        scores = [dot(k[h], q[h], (1, 1)) for h in range(HEADS)]
        d_probs = [dot(v[h], da[h], (1, 1)) for h in range(HEADS)]
        probs_b, d_scores = [], []
        for h in range(HEADS):
            x = (scores[h] * inv).reshape(FRAMES, 8, CHUNK)
            e = jnp.exp(x - jnp.max(x, 0, keepdims=True))
            probs = e * (kept / jnp.sum(e, 0, keepdims=True))
            probs_b.append(probs.astype(BF16).reshape(CHUNK, CHUNK))
            dp_ = d_probs[h].reshape(FRAMES, 8, CHUNK)
            spread = jnp.sum(probs * dp_, 0, keepdims=True)
            d_scores.append((probs * (dp_ - spread) * inv).astype(BF16).reshape(CHUNK, CHUNK))
        attended = [dot(probs_b[h], v[h], (0, 0)).astype(BF16) for h in range(HEADS)]
        d_q = [dot(d_scores[h], k[h], (0, 0)).astype(BF16) for h in range(HEADS)]
        d_k = [dot(d_scores[h], q[h], (1, 0)).astype(BF16) for h in range(HEADS)]
        d_v = [dot(probs_b[h], da[h], (1, 0)).astype(BF16) for h in range(HEADS)]
        for h in range(HEADS):
            att[at, h * HD:h * HD + HD] = attended[h]
            att_slots[at, h * SLOT_E:h * SLOT_E + HD] = attended[h]
            for part, grad in enumerate((d_q, d_k, d_v)):
                dqkv[at, cols[h][part]:cols[h][part] + HD] = grad[h]

    def back_copy(part, d):
        to = pl.ds(pl.multiple_of(lax.rem(spot + d, 8) * 16, 16), 16)
        at = slice(2 * part, 2 * part + 2)
        return remote(
            d_in.at[at, to, :], back.at[part, d], b_send.at[part, d], b_recv.at[part, d], peer(d)
        )

    for part_ in range(2):
        for d in range(1, 8):
            for copy in spread_copies(part_, d):
                copy.wait_recv()
        two = slice(2 * part_, 2 * part_ + 2)
        at = slice(part_ * HALF_ROWS, part_ * HALF_ROWS + HALF_ROWS)
        m = m_all[two].reshape(HALF_ROWS, WIDTH)
        qkv[at, :] = dot(m, wq_all[...], (1, 1)).astype(BF16)
        dbranch[at, :] = (gate * d_all[two].reshape(HALF_ROWS, WIDTH).astype(F32)).astype(BF16)
        datt[at, :] = dot(dbranch[at, :], wo_all[...], (1, 0)).astype(BF16)

        @pl.loop(2 * part_, 2 * part_ + 2)
        def _(c):
            attention(pl.ds(pl.multiple_of(c * CHUNK, CHUNK), CHUNK))

        for n in range(3):
            lanes = slice(n * 384, n * 384 + 384)
            grad = dot(dqkv[at, :], wq_all[:, lanes], (1, 0)).astype(BF16)
            d_in[two, :, lanes] = grad.reshape(2, CHUNK, 384)
        for d in range(1, 8):
            back_copy(part_, d).start()

    def block(size, z):
        return pl.ds(pl.multiple_of(z * size, 16), size)

    sizes = (BLOCK_Q, BLOCK_O)
    terms, theirs = (gq, go), (xq, xo)

    def pair_copy(i, n):
        at = block(sizes[n], lax.rem(clip + OFFSETS[i], 8))
        return remote(
            terms[n].at[1 - core, at, :], theirs[n].at[at, :], x_send.at[i, n], x_recv.at[i, n], twin
        )

    turned[...] = m_all[...].reshape(ROWS, WIDTH).T
    slots = att_slots[...].T

    def weight_terms(h):
        go[h] = dot(slots, dbranch[:, pl.ds(pl.multiple_of(h * START_O, 128), HALF_O)], (1, 0)).astype(BF16)
        for first, lanes in ((0, 512), (512, 384)):
            src = pl.ds(pl.multiple_of(h * HALF_Q + first, 128), lanes)
            gq[h, :, first:first + lanes] = dot(turned[...], dqkv[:, src], (1, 0)).astype(BF16)

    weight_terms(1 - core)
    for i in range(8):
        for n in range(2):
            pair_copy(i, n).start()
    weight_terms(core)

    def own(which, z, first, lanes):
        at = block(sizes[which], z)
        return (
            terms[which][core, at, first:first + lanes].astype(F32)
            + theirs[which][at, first:first + lanes].astype(F32)
        )

    def pieces(k, way):
        return FIRST_PIECES[way] if k == 0 else range(len(PIECES))

    def chain_copy(way, k, n):
        which, first, lanes = PIECES[n]
        src, dst = ((sq, rq), (so, ro))[which]
        return remote(
            src.at[way, k, :, first:first + lanes], dst.at[way, k, :, first:first + lanes],
            c_send.at[way, k, n], c_recv.at[way, k, n], along(1 if way == 0 else 7),
        )

    def arrived(way, k, n):
        which, first, lanes = PIECES[n]
        chain_copy(way, k, n).wait_recv()
        return (rq, ro)[which][way, k, :, first:first + lanes].astype(F32)

    def chain_step(k):
        for i in (0,) if k == 0 else (2 * k - 1, 2 * k):
            for n in range(2):
                pair_copy(i, n).wait_recv()
        for n in range(len(PIECES)):
            for way in range(2):
                if n not in pieces(k, way):
                    continue
                which, first, lanes = PIECES[n]
                z = lax.rem(clip + (4 - k if way == 0 else 4 + k), 8)
                total = own(which, z, first, lanes)
                if k and n in pieces(k - 1, way):
                    total = total + arrived(way, k - 1, n)
                (sq, so)[which][way, k, :, first:first + lanes] = total.astype(BF16)
                chain_copy(way, k, n).start()

    chain_step(0)

    gates = []
    for n in range(3):
        lanes = slice(n * 384, n * 384 + 384)
        branch = dot(att[...], wo_all[lanes, :], (1, 1))
        grads = d_all[:, :, lanes].reshape(ROWS, 384).astype(F32)
        gates.append(jnp.sum(branch * grads, 0, keepdims=True))
    part[2:3] = jnp.concatenate(gates, 1)
    part[3:] = jnp.zeros((5, WIDTH), F32)

    def tokens_back(half_):
        def step(d, carry):
            b = back[half_, d].astype(F32).reshape(32, WIDTH)
            b = jnp.stack(
                [
                    jnp.concatenate([b[16 * g + 8 * f:16 * g + 8 * f + 8] for g in range(2)], 0)
                    for f in range(2)
                ],
                0,
            )
            at = patches(half_, lax.rem(spot + 8 - d, 8))
            normed, rstd = normalise(tok[:, at, :].astype(F32))
            d_normed = b * scale
            one = jnp.mean(d_normed, -1, keepdims=True)
            two = jnp.mean(d_normed * normed, -1, keepdims=True)
            out = dout[:, at, :].astype(F32) + rstd * (d_normed - one - normed * two)
            dout[:, at, :] = out.astype(BF16)
            return (
                carry[0] + jnp.sum(b.reshape(4, 8, WIDTH), 0),
                carry[1] + jnp.sum((b * normed).reshape(4, 8, WIDTH), 0),
            )

        return step

    zero = jnp.zeros((8, WIDTH), F32)
    sums = (zero, zero)
    for part_ in range(2):
        back[part_, 0] = d_in[2 * part_:2 * part_ + 2, mine, :]
        for d in range(1, 8):
            back_copy(part_, d).wait_recv()
        sums = lax.fori_loop(0, 8, tokens_back(part_), sums)
        if part_ == 0:
            chain_step(1)
    result = pltpu.make_async_copy(dout, tok_out.at[0], here.at[4])
    result.start()
    part[0:1] = jnp.sum(sums[0], 0, keepdims=True)
    part[1:2] = jnp.sum(sums[1], 0, keepdims=True)

    def part_copy(d):
        return remote(part, parts.at[d], p_send.at[d], p_recv.at[d], peer(d))

    for d in range(1, 8):
        part_copy(d).start()
    chain_step(2)
    total = part[...]
    for d in range(1, 8):
        part_copy(d).wait_recv()
        total = total + parts[d]
    mods[clip] = total

    def mod_copy(d):
        ref = mods.at[clip]
        return remote(ref, ref, z_send.at[d], z_recv.at[d], along(d))

    for d in range(1, 8):
        mod_copy(d).start()
    chain_step(3)
    for n in range(2):
        pair_copy(7, n).wait_recv()
    sums_ = []
    for which in range(2):
        whole = []
        for n, (which_n, first, lanes) in enumerate(PIECES):
            if which_n == which:
                total = own(which, clip, first, lanes)
                for way in range(2):
                    total = total + arrived(way, 3, n)
                whole.append(total.astype(BF16))
        sums_.append(jnp.concatenate(whole, 1))

    def widen(x, size, slot):
        count = 8 * slot
        row = lax.broadcasted_iota(jnp.int32, (count, x.shape[0]), 0)
        col = lax.broadcasted_iota(jnp.int32, (count, x.shape[0]), 1)
        inside = lax.rem(row, slot)
        pick = jnp.logical_and(col == lax.div(row, slot) * size + inside, inside < size)
        return dot(pick.astype(F32).astype(BF16), x, (1, 0)).astype(BF16)

    wide_q, wide_o = widen(sums_[0], 18, 32), widen(sums_[1], 9, 16)
    for j in range(8):
        for low in range(2):
            stage[j, low, 0:32, :] = wide_q[32 * j:32 * j + 32, 384 * low:384 * low + 512]
            stage[j, low, 32:48, 0:384] = wide_o[16 * j:16 * j + 16, 256 * low:256 * low + 384]
            stage[j, low, 32:48, 384:512] = jnp.zeros((16, 128), BF16)

    def owner_copy(d, low):
        to = half * 8 + d
        return pltpu.make_async_remote_copy(
            src_ref=stage.at[lax.rem(spot + d, 8), low], dst_ref=final.at[to],
            send_sem=f_send.at[d, low], recv_sem=f_recv.at[to],
            device_id=owner(d, low), device_id_type=MESH,
        )

    for d in range(1, 8):
        for low in range(2):
            owner_copy(d, low).start()
    for low in range(2):
        is_self = jnp.logical_and(core == half, core == low)

        @pl.when(is_self)
        def _():
            pltpu.make_async_copy(stage.at[spot, low], final.at[half * 8], f_recv.at[half * 8]).start()

        @pl.when(jnp.logical_not(is_self))
        def _():
            owner_copy(0, low).start()

    for i in range(16):
        wait_bytes(final.at[i], f_recv.at[i])
    total = final[0].astype(F32)
    for i in range(1, 16):
        total = total + final[i].astype(F32)
    got_q = jnp.where(core == 0, total[0:32, 0:SHARD_Q], total[0:32, 48:48 + SHARD_Q])
    first_o = 64 * half + 32 * core
    got_o = total[32:48, 0:SHARD_O]
    for start in (32, 64, 96):
        got_o = jnp.where(first_o == start, total[32:48, start:start + SHARD_O], got_o)
    oq[...] = got_q[0:18]
    oo[...] = got_o[0:9]

    for d in range(1, 8):
        mod_copy(d).wait()
        part_copy(d).wait_send()
        for part_ in range(2):
            back_copy(part_, d).wait_send()
            for copy in spread_copies(part_, d):
                copy.wait_send()
        for low in range(2):
            owner_copy(d, low).wait_send()
    for low in range(2):
        @pl.when(jnp.logical_or(core != half, core != low))
        def _():
            owner_copy(0, low).wait_send()
    for n in range(2):
        own_copy(n).wait_send()
        for i in range(8):
            pair_copy(i, n).wait_send()
    for k in range(STEPS):
        for way in range(2):
            for n in pieces(k, way):
                chain_copy(way, k, n).wait_send()

    def sent(parity):
        for i in range(4):
            for n in range(2):
                across_copy(n, parity, i).wait_send()
                along_copy(n, parity, i).wait_send()
                twin_copy(n, parity, i, 0).wait_send()
                twin_copy(n, 1 - parity, i, 1).wait_send()

    by_parity(clip, sent)
    for i in range(3):
        d_mod[0, i] = jnp.concatenate([mods[z, i:i + 1] for z in range(8)], 0)
    result.wait()


def copy_kernel(*refs):
    count = len(refs) // 2
    for i in range(count):
        refs[count + i][...] = refs[i][...]


def body(tokens, d_out, modulation, w_qkv, w_out):
    dma = pltpu.SemaphoreType.DMA

    def held(*shape, dtype=BF16):
        return pltpu.VMEM(shape, dtype)

    anywhere = pl.BlockSpec(memory_space=pl.ANY)
    inside = pl.BlockSpec(memory_space=pltpu.VMEM)
    outs = [
        jax.ShapeDtypeStruct(tokens.shape, BF16),
        jax.ShapeDtypeStruct((1, 3, 8, WIDTH), F32),
        jax.ShapeDtypeStruct((18, SHARD_Q), F32),
        jax.ShapeDtypeStruct((9, SHARD_O), F32),
    ]
    chains = (2, STEPS, len(PIECES))
    results = pl.pallas_call(
        fused_kernel,
        out_shape=outs,
        in_specs=[anywhere, anywhere, inside, anywhere, anywhere],
        out_specs=[anywhere, inside, inside, inside],
        scratch_shapes=[
            held(2, 256, WIDTH), held(2, 256, WIDTH),
            held(2, 8, 2, 16, WIDTH), held(2, 8, 2, 16, WIDTH),
            held(CHUNKS, CHUNK, WIDTH), held(CHUNKS, CHUNK, WIDTH),
            held(2 * HALF_Q, WIDTH), held(WIDTH, HEADS * HD),
            held(ROWS, 2 * HALF_Q), held(ROWS, HEADS * HD), held(ROWS, HEADS * HD),
            held(ROWS, HEADS * SLOT_E), held(ROWS, WIDTH), held(ROWS, 2 * HALF_Q),
            held(WIDTH, ROWS), held(CHUNKS, CHUNK, WIDTH),
            held(2, WIDTH, HALF_Q), held(2, HEADS * SLOT_E, HALF_O),
            held(2, 8, 2, 16, WIDTH), held(WIDTH, HALF_Q), held(HEADS * SLOT_E, HALF_O),
            held(2, STEPS, BLOCK_Q, HALF_Q), held(2, STEPS, BLOCK_O, HALF_O),
            held(2, STEPS, BLOCK_Q, HALF_Q), held(2, STEPS, BLOCK_O, HALF_O),
            held(8, 2, 48, 512), held(16, 48, 512),
            held(8, WIDTH, dtype=F32), held(8, 8, WIDTH, dtype=F32), held(8, 8, WIDTH, dtype=F32),
            dma((5,)), dma((2, 2, 8)), dma((2, 2, 8)), dma((2,)), dma((2,)),
            dma((2, 4)), dma((2, 4)), dma((2, 4)), dma((2, 4)), dma((2, 4, 2)), dma((2, 4, 2)),
            dma((2, 8)), dma((2, 8)), dma((8, 2)), dma((8, 2)), dma(chains), dma(chains),
            dma((8,)), dma((8,)), dma((8,)), dma((8,)), dma((8, 2)), dma((16,)),
        ],
        compiler_params=pltpu.CompilerParams(
            vmem_limit_bytes=VMEM_BYTES, collective_id=0, has_side_effects=True
        ),
    )(tokens, d_out, jnp.swapaxes(modulation, 1, 2), w_qkv, w_out)
    d_tokens, d_mod, g_qkv, g_out = pl.pallas_call(
        copy_kernel,
        out_shape=outs,
        in_specs=[inside] * 4,
        out_specs=[inside] * 4,
        compiler_params=pltpu.CompilerParams(vmem_limit_bytes=16 * 1024 * 1024),
    )(*results)
    return d_tokens, jnp.swapaxes(d_mod, 1, 2), g_qkv.T, g_out.T


def solution(mesh):
    in_specs = (
        P("dp", "seq", None, None),
        P("dp", "seq", None, None),
        P("dp", None, None, None),
        P("dp", None),
        P("dp", None),
    )
    out_specs = (
        P("dp", "seq", None, None),
        P("dp", None, None, None),
        P("dp", "seq"),
        P("dp", "seq"),
    )
    return jax.shard_map(body, mesh=mesh, in_specs=in_specs, out_specs=out_specs, check_vma=False)
```

```python
import math

import jax
import jax.numpy as jnp
from jax import lax
from jax.experimental import pallas as pl
from jax.experimental.pallas import tpu as pltpu
from jax.sharding import PartitionSpec as P

MESH = pl.DeviceIdType.MESH
F32 = jnp.float32
BF16 = jnp.bfloat16

WIDTH = 1152
HEADS = 8
HD = 72
FRAMES = 16
CLIP_DEVICES = 8
CHUNKS = 4
CHUNK = 128
ROWS = 512
SHARD_Q = 432
SHARD_O = 288
HALF_Q = 896
HALF_O = 640
START_O = 512
SLOT_E = 80
EPS = 1e-06
VMEM_BYTES = 56 * 1024 * 1024

PIECES = ((0, 256), (256, 256), (512, 384))
FIRST_PIECES = ((0, 1), (2,))
BLOCK_Q = 144
PACKED = 512
OFFSETS = (4, 3, 5, 2, 6, 1, 7, 0)
STEPS = 4
HALF_ROWS = 256

PIECES_WQ = (((0, 64), (64, 48), (112, 64), (176, 48)), ((224, 64), (288, 48), (336, 48), (384, 48)))
PIECES_WO = (((0, 48), (48, 32), (80, 32), (112, 32)), ((144, 48), (192, 32), (224, 32), (256, 32)))


def dot(left, right, contract):
    return lax.dot_general(
        left, right, ((contract[:1], contract[1:]), ((), ())), preferred_element_type=F32
    )


def place():
    seq, dp = lax.axis_index("seq"), lax.axis_index("dp")
    clip, spot = lax.div(seq, 8), lax.rem(seq, 8)
    half, core = lax.div(dp, 2), lax.rem(dp, 2)
    return seq, dp, clip, spot, half, core


def column(part, head):
    block = part * HEADS + head
    return block * HD if block < 12 else HALF_Q + (block - 12) * HD


def normalise(x):
    center = x - jnp.mean(x, -1, keepdims=True)
    var = jnp.mean(center * center, -1, keepdims=True)
    rstd = lax.rsqrt(var + EPS)
    return center * rstd, rstd


def signal_all(barrier, devices):
    for device in devices:
        pl.semaphore_signal(barrier, inc=1, device_id=device, device_id_type=MESH)


def by_parity(clip, act):
    for parity in range(2):
        @pl.when(lax.rem(clip, 2) == parity)
        def _():
            act(parity)


def wait_bytes(ref, sem):
    pltpu.make_async_copy(ref, ref, sem).wait()


def fused_kernel(
    tok_in, dout_in, mod, wq, wo, tok_out, d_mod, oq, oo,
    tok, dout, m_send, d_send, m_all, d_all, wq_all, wo_all,
    qkv, datt, att, dbranch, dqkv, turned, d_in, gq, go,
    back, xq, xo, sq, rq, stage, final, stage_o, final_o, spread_o, last_o, part, parts, mods,
    here, a_send, a_recv, own_send, own_recv, w_send, w_recv, v_send, v_recv, t_send, t_recv,
    b_send, b_recv, x_send, x_recv, c_send, c_recv, p_send, p_recv,
    z_send, z_recv, f_send, f_recv, y_send, y_recv, o_send, o_recv, l_send, l_recv,
):
    seq, dp, clip, spot, half, core = place()
    twin = {"seq": seq, "dp": half * 2 + 1 - core}
    across = {
        "seq": clip * 8 + (1 - lax.div(spot, 4)) * 4 + lax.rem(spot, 4),
        "dp": (1 - half) * 2 + core,
    }

    def peer(d):
        return {"seq": clip * 8 + lax.rem(spot + d, 8), "dp": dp}

    def along(d):
        return {"seq": lax.rem(clip + d, 8) * 8 + spot, "dp": dp}

    def owner(d, low):
        return {"seq": clip * 8 + lax.rem(spot + d, 8), "dp": core * 2 + low}

    def source(d, h):
        return {"seq": clip * 8 + lax.rem(spot + 8 - d, 8), "dp": h * 2 + half}

    def remote(src, dst, send, recv, device):
        return pltpu.make_async_remote_copy(
            src_ref=src, dst_ref=dst, send_sem=send, recv_sem=recv,
            device_id=device, device_id_type=MESH,
        )

    loads = [
        pltpu.make_async_copy(tok_in.at[0], tok, here.at[0]),
        pltpu.make_async_copy(dout_in.at[0], dout, here.at[1]),
    ]
    for copy in loads:
        copy.start()
    barrier = pltpu.get_barrier_semaphore()
    signal_all(barrier, [twin, across] + [peer(d) for d in range(1, 8)] + [along(d) for d in range(1, 8)])
    signal_all(barrier, [source(d, h) for d in range(1, 8) for h in range(2)])
    for h in range(2):
        @pl.when(jnp.logical_or(half != core, h != half))
        def _():
            signal_all(barrier, [source(0, h)])

    shards, wholes = (wq, wo), (wq_all, wo_all)

    def first_row(n, h, c):
        return h * HALF_Q + c * SHARD_Q if n == 0 else (h * 2 + c) * SHARD_O

    def rows(n, h, c, at):
        return wholes[n].at[pl.ds(pl.multiple_of(first_row(n, h, c) + at[0], 16), at[1])]

    def entire(n):
        return (0, (SHARD_Q, SHARD_O)[n])

    def piece(n, parity, i):
        return (PIECES_WQ, PIECES_WO)[n][parity][i]

    def own_copy(n):
        return remote(shards[n], rows(n, half, core, entire(n)), own_send.at[n], own_recv.at[n], twin)

    def keep_copy(n):
        return pltpu.make_async_copy(shards[n], rows(n, half, core, entire(n)), here.at[2 + n])

    def across_copy(n, parity, i):
        at = piece(n, parity, i)
        return remote(
            shards[n].at[pl.ds(at[0], at[1])], rows(n, half, core, at),
            w_send.at[n, i], w_recv.at[n, i], across,
        )

    def passed(n, parity, i):
        return rows(n, 1 - half, core, piece(n, parity, i))

    def along_copy(n, parity, i):
        ref = passed(n, parity, i)
        return remote(ref, ref, v_send.at[n, i], v_recv.at[n, i], along(1 if i % 2 == 0 else 7))

    def twin_copy(n, parity, i, own):
        ref = passed(n, parity, i)
        return remote(ref, ref, t_send.at[n, i, own], t_recv.at[n, i, own], twin)

    def send_across(parity):
        for i in range(4):
            for n in range(2):
                across_copy(n, parity, i).start()

    zeros = jnp.zeros((HALF_Q - 2 * SHARD_Q, WIDTH), BF16)
    wq_all[2 * SHARD_Q:HALF_Q, :] = zeros
    wq_all[HALF_Q + 2 * SHARD_Q:, :] = zeros

    own_mod = mod[0, :, pl.ds(clip, 1), :].reshape(3, WIDTH)
    shift, scale, gate = own_mod[0:1], 1.0 + own_mod[1:2], own_mod[2:3]
    mine = pl.ds(pl.multiple_of(spot * 16, 16), 16)

    def arranged(x):
        return jnp.concatenate(
            [x[f, 8 * g:8 * g + 8] for g in range(2) for f in range(2)], 0
        ).astype(BF16).reshape(2, 16, WIDTH)

    def patches(part, j):
        return pl.ds(pl.multiple_of(j * 32 + part * 16, 16), 16)

    def blocks(part, d):
        at = patches(part, lax.rem(spot + d, 8))
        normed, _ = normalise(tok[:, at, :].astype(F32))
        return arranged(normed * scale + shift), arranged(dout[:, at, :].astype(F32))

    def spread_copies(part, d):
        return [
            remote(
                src.at[part, d], dst.at[2 * part:2 * part + 2, mine, :],
                a_send.at[i, part, d], a_recv.at[i, part, d], peer(d),
            )
            for i, (src, dst) in enumerate(((m_send, m_all), (d_send, d_all)))
        ]

    for n in range(2):
        keep_copy(n).start()
    for copy in loads:
        copy.wait()

    def prepare(part, d):
        m_send[part, d], d_send[part, d] = blocks(part, d)

    def prepare_step(part):
        def step(d, carry):
            prepare(part, d)
            return carry

        return step

    lax.fori_loop(0, 8, prepare_step(0), 0, unroll=2)
    pl.semaphore_wait(barrier, jnp.where(half == core, 31, 32))
    by_parity(clip, send_across)

    @pl.loop(1, 8)
    def _(d):
        for copy in spread_copies(0, d):
            copy.start()

    for n in range(2):
        own_copy(n).start()

    @pl.loop(1, 8)
    def _(d):
        prepare(1, d)
        for copy in spread_copies(1, d):
            copy.start()

    prepare(1, 0)
    for part_ in range(2):
        at = slice(2 * part_, 2 * part_ + 2)
        m_all[at, mine, :], d_all[at, mine, :] = m_send[part_, 0], d_send[part_, 0]

    for start in (2 * SHARD_Q, HALF_Q + 2 * SHARD_Q):
        dqkv[:, start:start + 32] = jnp.zeros((ROWS, 32), BF16)

    for i in range(4):
        def hand_on(parity):
            for n in range(2):
                across_copy(n, parity, i).wait_recv()
                along_copy(n, parity, i).start()
                twin_copy(n, parity, i, 0).start()

        by_parity(clip, hand_on)
    for i in range(4):
        def hand_twin(parity):
            for n in range(2):
                along_copy(n, 1 - parity, i).wait_recv()
                twin_copy(n, 1 - parity, i, 1).start()

        by_parity(clip, hand_twin)
    for n in range(2):
        keep_copy(n).wait()
        own_copy(n).wait_recv()

    def from_twin(parity):
        for i in range(4):
            for n in range(2):
                twin_copy(n, parity, i, 0).wait_recv()
                twin_copy(n, 1 - parity, i, 1).wait_recv()

    by_parity(clip, from_twin)

    inv = 1.0 / math.sqrt(HD)
    kept = (
        lax.broadcasted_iota(jnp.int32, (1, 8, CHUNK), 1)
        == lax.rem(lax.broadcasted_iota(jnp.int32, (1, 8, CHUNK), 2), 8)
    ).astype(F32)

    def attention(at):
        cols = [[column(part, h) for part in range(3)] for h in range(HEADS)]
        q, k, v = (
            [qkv[at, cols[h][part]:cols[h][part] + HD] for h in range(HEADS)] for part in range(3)
        )
        da = [datt[at, h * HD:h * HD + HD] for h in range(HEADS)]
        scores = [dot(k[h], q[h], (1, 1)) for h in range(HEADS)]
        d_probs = [dot(v[h], da[h], (1, 1)) for h in range(HEADS)]
        probs_b, d_scores = [], []
        for h in range(HEADS):
            x = (scores[h] * inv).reshape(FRAMES, 8, CHUNK)
            e = jnp.exp(x - jnp.max(x, 0, keepdims=True))
            probs = e * (kept / jnp.sum(e, 0, keepdims=True))
            probs_b.append(probs.astype(BF16).reshape(CHUNK, CHUNK))
            dp_ = d_probs[h].reshape(FRAMES, 8, CHUNK)
            spread = jnp.sum(probs * dp_, 0, keepdims=True)
            d_scores.append((probs * (dp_ - spread) * inv).astype(BF16).reshape(CHUNK, CHUNK))
        attended = [dot(probs_b[h], v[h], (0, 0)).astype(BF16) for h in range(HEADS)]
        d_q = [dot(d_scores[h], k[h], (0, 0)).astype(BF16) for h in range(HEADS)]
        d_k = [dot(d_scores[h], q[h], (1, 0)).astype(BF16) for h in range(HEADS)]
        d_v = [dot(probs_b[h], da[h], (1, 0)).astype(BF16) for h in range(HEADS)]
        for h in range(HEADS):
            att[at, h * HD:h * HD + HD] = attended[h]
            for part, grad in enumerate((d_q, d_k, d_v)):
                dqkv[at, cols[h][part]:cols[h][part] + HD] = grad[h]

    def back_copy(part, d):
        to = pl.ds(pl.multiple_of(lax.rem(spot + d, 8) * 16, 16), 16)
        at = slice(2 * part, 2 * part + 2)
        return remote(
            d_in.at[at, to, :], back.at[part, d], b_send.at[part, d], b_recv.at[part, d], peer(d)
        )

    for part_ in range(2):
        for d in range(1, 8):
            for copy in spread_copies(part_, d):
                copy.wait_recv()
        two = slice(2 * part_, 2 * part_ + 2)
        at = slice(part_ * HALF_ROWS, part_ * HALF_ROWS + HALF_ROWS)
        m = m_all[two].reshape(HALF_ROWS, WIDTH)
        qkv[at, :] = dot(m, wq_all[...], (1, 1)).astype(BF16)
        dbranch[at, :] = (gate * d_all[two].reshape(HALF_ROWS, WIDTH).astype(F32)).astype(BF16)
        datt[at, :] = dot(dbranch[at, :], wo_all[...], (1, 0)).astype(BF16)

        @pl.loop(2 * part_, 2 * part_ + 2)
        def _(c):
            attention(pl.ds(pl.multiple_of(c * CHUNK, CHUNK), CHUNK))

        for n in range(3):
            lanes = slice(n * 384, n * 384 + 384)
            grad = dot(dqkv[at, :], wq_all[:, lanes], (1, 0)).astype(BF16)
            d_in[two, :, lanes] = grad.reshape(2, CHUNK, 384)
        for d in range(1, 8):
            back_copy(part_, d).start()

    def block(size, z):
        return pl.ds(pl.multiple_of(z * size, 16), size)

    def pair_copy(i):
        at = block(BLOCK_Q, lax.rem(clip + OFFSETS[i], 8))
        return remote(gq.at[1 - core, at, :], xq.at[at, :], x_send.at[i], x_recv.at[i], twin)

    def pair_copy_o():
        return remote(go.at[1 - core], xo, y_send, y_recv, twin)

    slot = lax.broadcasted_iota(jnp.int32, (HEADS * SLOT_E, HEADS * HD), 0)
    inner = lax.rem(slot, SLOT_E)
    from_ = lax.div(inner, 9) * HD + lax.div(slot, SLOT_E) * 9 + lax.rem(inner, 9)
    pick = jnp.logical_and(
        lax.broadcasted_iota(jnp.int32, (HEADS * SLOT_E, HEADS * HD), 1) == from_, inner < HD
    )
    slots = dot(pick.astype(F32).astype(BF16), att[...], (1, 1)).astype(BF16)

    def out_terms(h):
        go[h] = dot(slots, dbranch[:, pl.ds(pl.multiple_of(h * START_O, 128), HALF_O)], (1, 0)).astype(BF16)

    def qkv_terms(h):
        for first, lanes in ((0, 512), (512, 384)):
            src = pl.ds(pl.multiple_of(h * HALF_Q + first, 128), lanes)
            gq[h, :, first:first + lanes] = dot(turned[...], dqkv[:, src], (1, 0)).astype(BF16)

    def plane_sends(copy, keep):
        for d in range(1, 8):
            for low in range(2):
                copy(d, low).start()
        for low in range(2):
            is_self = jnp.logical_and(core == half, core == low)

            @pl.when(is_self)
            def _():
                keep(low).start()

            @pl.when(jnp.logical_not(is_self))
            def _():
                copy(0, low).start()

    def plane_sent(copy):
        for d in range(1, 8):
            for low in range(2):
                copy(d, low).wait_send()
        for low in range(2):
            @pl.when(jnp.logical_or(core != half, core != low))
            def _():
                copy(0, low).wait_send()

    def plane_o(d, low):
        to = half * 8 + d
        return remote(
            stage_o.at[lax.rem(spot + d, 8), :, 256 * low:256 * low + 384], final_o.at[to],
            o_send.at[d, low], o_recv.at[to], owner(d, low),
        )

    def keep_o(low):
        return pltpu.make_async_copy(
            stage_o.at[spot, :, 256 * low:256 * low + 384], final_o.at[half * 8], o_recv.at[half * 8]
        )

    out_terms(1 - core)
    pair_copy_o().start()
    out_terms(core)
    turned[...] = m_all[...].reshape(ROWS, WIDTH).T
    qkv_terms(1 - core)
    for i in range(8):
        pair_copy(i).start()
    pair_copy_o().wait_recv()
    for j in range(8):
        at = slice(SLOT_E * j, SLOT_E * j + SLOT_E)
        stage_o[j] = (go[core, at, :].astype(F32) + xo[at, :].astype(F32)).astype(BF16)
    plane_sends(plane_o, keep_o)
    qkv_terms(core)

    def own(z, first, lanes):
        at = block(BLOCK_Q, z)
        return (
            gq[core, at, first:first + lanes].astype(F32) + xq[at, first:first + lanes].astype(F32)
        )

    def pieces(k, way):
        return FIRST_PIECES[way] if k == 0 else range(len(PIECES))

    def chain_copy(way, k, n):
        first, lanes = PIECES[n]
        return remote(
            sq.at[way, k, :, first:first + lanes], rq.at[way, k, :, first:first + lanes],
            c_send.at[way, k, n], c_recv.at[way, k, n], along(1 if way == 0 else 7),
        )

    def arrived(way, k, n):
        first, lanes = PIECES[n]
        chain_copy(way, k, n).wait_recv()
        return rq[way, k, :, first:first + lanes].astype(F32)

    def chain_step(k):
        for i in (0,) if k == 0 else (2 * k - 1, 2 * k):
            pair_copy(i).wait_recv()
        for n in range(len(PIECES)):
            for way in range(2):
                if n not in pieces(k, way):
                    continue
                first, lanes = PIECES[n]
                z = lax.rem(clip + (4 - k if way == 0 else 4 + k), 8)
                total = own(z, first, lanes)
                if k and n in pieces(k - 1, way):
                    total = total + arrived(way, k - 1, n)
                sq[way, k, :, first:first + lanes] = total.astype(BF16)
                chain_copy(way, k, n).start()

    chain_step(0)

    gates = []
    for n in range(3):
        lanes = slice(n * 384, n * 384 + 384)
        branch = dot(att[...], wo_all[lanes, :], (1, 1))
        grads = d_all[:, :, lanes].reshape(ROWS, 384).astype(F32)
        gates.append(jnp.sum(branch * grads, 0, keepdims=True))
    gate_row = jnp.concatenate(gates, 1)

    def tokens_back(half_):
        def step(d, carry):
            b = back[half_, d].astype(F32).reshape(32, WIDTH)
            b = jnp.stack(
                [
                    jnp.concatenate([b[16 * g + 8 * f:16 * g + 8 * f + 8] for g in range(2)], 0)
                    for f in range(2)
                ],
                0,
            )
            at = patches(half_, lax.rem(spot + 8 - d, 8))
            normed, rstd = normalise(tok[:, at, :].astype(F32))
            d_normed = b * scale
            one = jnp.mean(d_normed, -1, keepdims=True)
            two = jnp.mean(d_normed * normed, -1, keepdims=True)
            out = dout[:, at, :].astype(F32) + rstd * (d_normed - one - normed * two)
            dout[:, at, :] = out.astype(BF16)
            return (
                carry[0] + jnp.sum(b.reshape(4, 8, WIDTH), 0),
                carry[1] + jnp.sum((b * normed).reshape(4, 8, WIDTH), 0),
            )

        return step

    zero = jnp.zeros((8, WIDTH), F32)
    sums = (zero, zero)
    for part_ in range(2):
        back[part_, 0] = d_in[2 * part_:2 * part_ + 2, mine, :]
        for d in range(1, 8):
            back_copy(part_, d).wait_recv()
        sums = lax.fori_loop(0, 8, tokens_back(part_), sums, unroll=2)
        if part_ == 0:
            chain_step(1)
    result = pltpu.make_async_copy(dout, tok_out.at[0], here.at[4])
    result.start()
    flat = jnp.concatenate(
        [jnp.sum(sums[0], 0, keepdims=True), jnp.sum(sums[1], 0, keepdims=True), gate_row,
         jnp.zeros((1, 8 * PACKED - 3 * WIDTH), F32)], 1
    )
    part[...] = jnp.concatenate([flat[:, PACKED * i:PACKED * i + PACKED] for i in range(8)], 0)

    def part_copy(d):
        return remote(part, parts.at[d], p_send.at[d], p_recv.at[d], peer(d))

    for d in range(1, 8):
        part_copy(d).start()
    chain_step(2)

    def widen(x, size, slot):
        count = 8 * slot
        row = lax.broadcasted_iota(jnp.int32, (count, x.shape[0]), 0)
        col = lax.broadcasted_iota(jnp.int32, (count, x.shape[0]), 1)
        inside = lax.rem(row, slot)
        pick = jnp.logical_and(col == lax.div(row, slot) * size + inside, inside < size)
        return dot(pick.astype(F32).astype(BF16), x, (1, 0)).astype(BF16)

    def plane_sum(ref, sems):
        for i in range(16):
            wait_bytes(ref.at[i], sems.at[i])
        total = ref[0].astype(F32)
        for i in range(1, 16):
            total = total + ref[i].astype(F32)
        return total

    def last_copy(d):
        return remote(
            spread_o.at[lax.rem(clip + d, 8)], last_o.at[d], l_send.at[d], l_recv.at[d], along(d)
        )

    spread_o[...] = widen(plane_sum(final_o, o_recv).astype(BF16), 9, 16).reshape(8, 16, 384)
    for d in range(1, 8):
        last_copy(d).start()
    total = part[...]
    for d in range(1, 8):
        part_copy(d).wait_recv()
        total = total + parts[d]
    mods[clip] = total

    def mod_copy(d):
        ref = mods.at[clip]
        return remote(ref, ref, z_send.at[d], z_recv.at[d], along(d))

    for d in range(1, 8):
        mod_copy(d).start()
    chain_step(3)
    pair_copy(7).wait_recv()
    whole = []
    for n, (first, lanes) in enumerate(PIECES):
        total = own(clip, first, lanes)
        for way in range(2):
            total = total + arrived(way, 3, n)
        whole.append(total.astype(BF16))
    wide = widen(jnp.concatenate(whole, 1), 18, 32)
    for j in range(8):
        for low in range(2):
            stage[j, low] = wide[32 * j:32 * j + 32, 384 * low:384 * low + 512]

    def plane_q(d, low):
        to = half * 8 + d
        return remote(
            stage.at[lax.rem(spot + d, 8), low], final.at[to],
            f_send.at[d, low], f_recv.at[to], owner(d, low),
        )

    def keep_q(low):
        return pltpu.make_async_copy(stage.at[spot, low], final.at[half * 8], f_recv.at[half * 8])

    plane_sends(plane_q, keep_q)
    total = spread_o[clip].astype(F32)
    for d in range(1, 8):
        last_copy(d).wait_recv()
        total = total + last_o[d].astype(F32)
    first_o = 64 * half + 32 * core
    got_o = total[:, 0:SHARD_O]
    for start in (32, 64, 96):
        got_o = jnp.where(first_o == start, total[:, start:start + SHARD_O], got_o)
    oo[...] = got_o[0:9]
    for d in range(1, 8):
        mod_copy(d).wait()
    flats = [jnp.concatenate([mods[z, i:i + 1] for i in range(8)], 1) for z in range(8)]
    for i in range(3):
        d_mod[0, i] = jnp.concatenate([flat[:, WIDTH * i:WIDTH * i + WIDTH] for flat in flats], 0)
    total = plane_sum(final, f_recv)
    got_q = jnp.where(core == 0, total[:, 0:SHARD_Q], total[:, 48:48 + SHARD_Q])
    oq[...] = got_q[0:18]

    plane_sent(plane_o)
    plane_sent(plane_q)
    for d in range(1, 8):
        last_copy(d).wait_send()
        part_copy(d).wait_send()
        for part_ in range(2):
            back_copy(part_, d).wait_send()
            for copy in spread_copies(part_, d):
                copy.wait_send()
    pair_copy_o().wait_send()
    for n in range(2):
        own_copy(n).wait_send()
    for i in range(8):
        pair_copy(i).wait_send()
    for k in range(STEPS):
        for way in range(2):
            for n in pieces(k, way):
                chain_copy(way, k, n).wait_send()

    def sent(parity):
        for i in range(4):
            for n in range(2):
                across_copy(n, parity, i).wait_send()
                along_copy(n, parity, i).wait_send()
                twin_copy(n, parity, i, 0).wait_send()
                twin_copy(n, 1 - parity, i, 1).wait_send()

    by_parity(clip, sent)
    result.wait()


def copy_kernel(*refs):
    count = (len(refs) - 1) // 2
    copies = [
        pltpu.make_async_copy(refs[i], refs[count + i], refs[-1].at[i]) for i in range(count)
    ]
    for copy in copies:
        copy.start()
    for copy in copies:
        copy.wait()


def body(tokens, d_out, modulation, w_qkv, w_out):
    dma = pltpu.SemaphoreType.DMA

    def held(*shape, dtype=BF16):
        return pltpu.VMEM(shape, dtype)

    anywhere = pl.BlockSpec(memory_space=pl.ANY)
    inside = pl.BlockSpec(memory_space=pltpu.VMEM)
    outs = [
        jax.ShapeDtypeStruct(tokens.shape, BF16),
        jax.ShapeDtypeStruct((1, 3, 8, WIDTH), F32),
        jax.ShapeDtypeStruct((18, SHARD_Q), F32),
        jax.ShapeDtypeStruct((9, SHARD_O), F32),
    ]
    chains = (2, STEPS, len(PIECES))
    results = pl.pallas_call(
        fused_kernel,
        out_shape=outs,
        in_specs=[anywhere, anywhere, inside, anywhere, anywhere],
        out_specs=[anywhere, inside, inside, inside],
        scratch_shapes=[
            held(2, 256, WIDTH), held(2, 256, WIDTH),
            held(2, 8, 2, 16, WIDTH), held(2, 8, 2, 16, WIDTH),
            held(CHUNKS, CHUNK, WIDTH), held(CHUNKS, CHUNK, WIDTH),
            held(2 * HALF_Q, WIDTH), held(WIDTH, HEADS * HD),
            held(ROWS, 2 * HALF_Q), held(ROWS, HEADS * HD), held(ROWS, HEADS * HD),
            held(ROWS, WIDTH), held(ROWS, 2 * HALF_Q),
            held(WIDTH, ROWS), held(CHUNKS, CHUNK, WIDTH),
            held(2, WIDTH, HALF_Q), held(2, HEADS * SLOT_E, HALF_O),
            held(2, 8, 2, 16, WIDTH), held(WIDTH, HALF_Q), held(HEADS * SLOT_E, HALF_O),
            held(2, STEPS, BLOCK_Q, HALF_Q), held(2, STEPS, BLOCK_Q, HALF_Q),
            held(8, 2, 32, 512), held(16, 32, 512), held(8, SLOT_E, HALF_O), held(16, SLOT_E, 384),
            held(8, 16, 384), held(8, 16, 384),
            held(8, PACKED, dtype=F32), held(8, 8, PACKED, dtype=F32), held(8, 8, PACKED, dtype=F32),
            dma((5,)), dma((2, 2, 8)), dma((2, 2, 8)), dma((2,)), dma((2,)),
            dma((2, 4)), dma((2, 4)), dma((2, 4)), dma((2, 4)), dma((2, 4, 2)), dma((2, 4, 2)),
            dma((2, 8)), dma((2, 8)), dma((8,)), dma((8,)), dma(chains), dma(chains),
            dma((8,)), dma((8,)), dma((8,)), dma((8,)), dma((8, 2)), dma((16,)),
            dma, dma, dma((8, 2)), dma((16,)), dma((8,)), dma((8,)),
        ],
        compiler_params=pltpu.CompilerParams(
            vmem_limit_bytes=VMEM_BYTES, collective_id=0, has_side_effects=True
        ),
    )(tokens, d_out, jnp.swapaxes(modulation, 1, 2), w_qkv, w_out)
    d_tokens, d_mod, g_qkv, g_out = pl.pallas_call(
        copy_kernel,
        out_shape=outs,
        in_specs=[anywhere] * 4,
        out_specs=[inside] * 4,
        scratch_shapes=[dma((4,))],
        compiler_params=pltpu.CompilerParams(vmem_limit_bytes=VMEM_BYTES),
    )(*results)
    return d_tokens, jnp.swapaxes(d_mod, 1, 2), g_qkv.T, g_out.T


def solution(mesh):
    in_specs = (
        P("dp", "seq", None, None),
        P("dp", "seq", None, None),
        P("dp", None, None, None),
        P("dp", None),
        P("dp", None),
    )
    out_specs = (
        P("dp", "seq", None, None),
        P("dp", None, None, None),
        P("dp", "seq"),
        P("dp", "seq"),
    )
    return jax.shard_map(body, mesh=mesh, in_specs=in_specs, out_specs=out_specs, check_vma=False)
```

```python
import math

import jax
import jax.numpy as jnp
from jax import lax
from jax.experimental import pallas as pl
from jax.experimental.pallas import tpu as pltpu
from jax.sharding import PartitionSpec as P

MESH = pl.DeviceIdType.MESH
F32 = jnp.float32
BF16 = jnp.bfloat16

WIDTH = 1152
HEADS = 8
HD = 72
FRAMES = 16
CLIP_DEVICES = 8
CHUNKS = 4
CHUNK = 128
ROWS = 512
SHARD_Q = 432
SHARD_O = 288
HALF_Q = 896
HALF_O = 640
START_O = 512
SLOT_E = 80
EPS = 1e-06
VMEM_BYTES = 56 * 1024 * 1024

PIECES = ((0, 256), (256, 256), (512, 256))
FIRST_PIECES = ((0,), (1, 2))
CHAIN_LANES = 768
PLANE_LANES = 128
FINAL_LANES = 512
HIGH_LANES = CHAIN_LANES - 384
HIGH_FIRST = HIGH_LANES - 48
BLOCK_Q = 144
PACKED = 512

OFFSETS = (4, 3, 5, 2, 6, 1, 7, 0)
STEPS = 4
HALF_ROWS = 256

PIECES_WQ = (((0, 64), (64, 48), (112, 64), (176, 48)), ((224, 64), (288, 48), (336, 48), (384, 48)))
PIECES_WO = (((0, 48), (48, 32), (80, 32), (112, 32)), ((144, 48), (192, 32), (224, 32), (256, 32)))


def dot(left, right, contract):
    return lax.dot_general(
        left, right, ((contract[:1], contract[1:]), ((), ())), preferred_element_type=F32
    )


def place():
    seq, dp = lax.axis_index("seq"), lax.axis_index("dp")
    clip, spot = lax.div(seq, 8), lax.rem(seq, 8)
    half, core = lax.div(dp, 2), lax.rem(dp, 2)
    return seq, dp, clip, spot, half, core


def column(part, head):
    block = part * HEADS + head
    return block * HD if block < 12 else HALF_Q + (block - 12) * HD


def normalise(x):
    center = x - jnp.mean(x, -1, keepdims=True)
    var = jnp.mean(center * center, -1, keepdims=True)
    rstd = lax.rsqrt(var + EPS)
    return center * rstd, rstd


def signal_all(barrier, devices):
    for device in devices:
        pl.semaphore_signal(barrier, inc=1, device_id=device, device_id_type=MESH)


def by_parity(clip, act):
    for parity in range(2):
        @pl.when(lax.rem(clip, 2) == parity)
        def _():
            act(parity)


def wait_bytes(ref, sem):
    pltpu.make_async_copy(ref, ref, sem).wait()


def fused_kernel(
    tok_in, dout_in, mod, wq, wo, tok_out, d_mod, oq, oo,
    tok, dout, m_send, d_send, m_all, d_all, wq_all, wo_all,
    qkv, datt, att, dbranch, dqkv, turned, turned_p, perm, d_in, gq, gp, go,
    back, xq, xp, xo, sq, rq, stage, final, stage_p, final_p, spread_p, last_p, stage_o, final_o, spread_o, last_o, part, parts, mods,
    here, a_send, a_recv, own_send, own_recv, w_send, w_recv, v_send, v_recv, t_send, t_recv,
    b_send, b_recv, x_send, x_recv, c_send, c_recv, p_send, p_recv,
    z_send, z_recv, f_send, f_recv, y_send, y_recv, o_send, o_recv, l_send, l_recv,
    yp_send, yp_recv, op_send, op_recv, lp_send, lp_recv,
):
    seq, dp, clip, spot, half, core = place()
    twin = {"seq": seq, "dp": half * 2 + 1 - core}
    across = {
        "seq": clip * 8 + (1 - lax.div(spot, 4)) * 4 + lax.rem(spot, 4),
        "dp": (1 - half) * 2 + core,
    }

    def peer(d):
        return {"seq": clip * 8 + lax.rem(spot + d, 8), "dp": dp}

    def along(d):
        return {"seq": lax.rem(clip + d, 8) * 8 + spot, "dp": dp}

    def owner(d, low):
        return {"seq": clip * 8 + lax.rem(spot + d, 8), "dp": core * 2 + low}

    def source(d, h):
        return {"seq": clip * 8 + lax.rem(spot + 8 - d, 8), "dp": h * 2 + half}

    def remote(src, dst, send, recv, device):
        return pltpu.make_async_remote_copy(
            src_ref=src, dst_ref=dst, send_sem=send, recv_sem=recv,
            device_id=device, device_id_type=MESH,
        )

    loads = [
        pltpu.make_async_copy(tok_in.at[0], tok, here.at[0]),
        pltpu.make_async_copy(dout_in.at[0], dout, here.at[1]),
    ]
    for copy in loads:
        copy.start()
    barrier = pltpu.get_barrier_semaphore()
    signal_all(barrier, [twin, across] + [peer(d) for d in range(1, 8)] + [along(d) for d in range(1, 8)])
    signal_all(barrier, [source(d, h) for d in range(1, 8) for h in range(2)])
    for h in range(2):
        @pl.when(jnp.logical_or(half != core, h != half))
        def _():
            signal_all(barrier, [source(0, h)])

    shards, wholes = (wq, wo), (wq_all, wo_all)

    def first_row(n, h, c):
        return h * HALF_Q + c * SHARD_Q if n == 0 else (h * 2 + c) * SHARD_O

    def rows(n, h, c, at):
        return wholes[n].at[pl.ds(pl.multiple_of(first_row(n, h, c) + at[0], 16), at[1])]

    def entire(n):
        return (0, (SHARD_Q, SHARD_O)[n])

    def piece(n, parity, i):
        return (PIECES_WQ, PIECES_WO)[n][parity][i]

    def own_copy(n):
        return remote(shards[n], rows(n, half, core, entire(n)), own_send.at[n], own_recv.at[n], twin)

    def keep_copy(n):
        return pltpu.make_async_copy(shards[n], rows(n, half, core, entire(n)), here.at[2 + n])

    def across_copy(n, parity, i):
        at = piece(n, parity, i)
        return remote(
            shards[n].at[pl.ds(at[0], at[1])], rows(n, half, core, at),
            w_send.at[n, i], w_recv.at[n, i], across,
        )

    def passed(n, parity, i):
        return rows(n, 1 - half, core, piece(n, parity, i))

    def along_copy(n, parity, i):
        ref = passed(n, parity, i)
        return remote(ref, ref, v_send.at[n, i], v_recv.at[n, i], along(1 if i % 2 == 0 else 7))

    def twin_copy(n, parity, i, own):
        ref = passed(n, parity, i)
        return remote(ref, ref, t_send.at[n, i, own], t_recv.at[n, i, own], twin)

    def send_across(parity):
        for i in range(4):
            for n in range(2):
                across_copy(n, parity, i).start()

    zeros = jnp.zeros((HALF_Q - 2 * SHARD_Q, WIDTH), BF16)
    wq_all[2 * SHARD_Q:HALF_Q, :] = zeros
    wq_all[HALF_Q + 2 * SHARD_Q:, :] = zeros

    own_mod = mod[0, :, pl.ds(clip, 1), :].reshape(3, WIDTH)
    shift, scale, gate = own_mod[0:1], 1.0 + own_mod[1:2], own_mod[2:3]
    mine = pl.ds(pl.multiple_of(spot * 16, 16), 16)

    def arranged(x):
        return jnp.concatenate(
            [x[f, 8 * g:8 * g + 8] for g in range(2) for f in range(2)], 0
        ).astype(BF16).reshape(2, 16, WIDTH)

    def patches(part, j):
        return pl.ds(pl.multiple_of(j * 32 + part * 16, 16), 16)

    def blocks(part, d):
        at = patches(part, lax.rem(spot + d, 8))
        normed, _ = normalise(tok[:, at, :].astype(F32))
        return arranged(normed * scale + shift), arranged(dout[:, at, :].astype(F32))

    def spread_copy(i, part, d):
        src, dst = ((m_send, m_all), (d_send, d_all))[i]
        return remote(
            src.at[part, d], dst.at[2 * part:2 * part + 2, mine, :],
            a_send.at[i, part, d], a_recv.at[i, part, d], peer(d),
        )

    def spread(i, part):
        @pl.loop(1, 8)
        def _(d):
            spread_copy(i, part, d).start()

    for n in range(2):
        keep_copy(n).start()
    for copy in loads:
        copy.wait()

    def prepare(part, d):
        m_send[part, d], d_send[part, d] = blocks(part, d)

    def prepare_step(part):
        def step(d, carry):
            prepare(part, d)
            return carry

        return step

    lax.fori_loop(0, 8, prepare_step(0), 0, unroll=2)
    pl.semaphore_wait(barrier, jnp.where(half == core, 31, 32))
    by_parity(clip, send_across)

    spread(0, 0)
    spread(1, 0)
    for n in range(2):
        own_copy(n).start()

    @pl.loop(1, 8)
    def _(d):
        prepare(1, d)
        spread_copy(0, 1, d).start()

    prepare(1, 0)
    for part_ in range(2):
        at = slice(2 * part_, 2 * part_ + 2)
        m_all[at, mine, :], d_all[at, mine, :] = m_send[part_, 0], d_send[part_, 0]

    for start in (2 * SHARD_Q, HALF_Q + 2 * SHARD_Q):
        dqkv[:, start:start + 32] = jnp.zeros((ROWS, 32), BF16)

    for i in range(4):
        def hand_on(parity):
            for n in range(2):
                across_copy(n, parity, i).wait_recv()
                along_copy(n, parity, i).start()
                twin_copy(n, parity, i, 0).start()

        by_parity(clip, hand_on)
        if i == 1:
            spread(1, 1)
    @pl.loop(0, 9)
    def _(n):
        row = lax.broadcasted_iota(jnp.int32, (128, 1), 0) + n * 128
        inner = lax.rem(row, BLOCK_Q)
        from_ = lax.div(inner, 18) * BLOCK_Q + lax.div(row, BLOCK_Q) * 18 + lax.rem(inner, 18)
        found = lax.broadcasted_iota(jnp.int32, (128, WIDTH), 1) == from_
        perm[pl.ds(pl.multiple_of(n * 128, 128), 128), :] = found.astype(F32).astype(BF16)

    for i in range(4):
        def hand_twin(parity):
            for n in range(2):
                along_copy(n, 1 - parity, i).wait_recv()
                twin_copy(n, 1 - parity, i, 1).start()

        by_parity(clip, hand_twin)
    for n in range(2):
        keep_copy(n).wait()
        own_copy(n).wait_recv()

    def from_twin(parity):
        for i in range(4):
            for n in range(2):
                twin_copy(n, parity, i, 0).wait_recv()
                twin_copy(n, 1 - parity, i, 1).wait_recv()

    by_parity(clip, from_twin)

    inv = 1.0 / math.sqrt(HD)
    kept = (
        lax.broadcasted_iota(jnp.int32, (1, 8, CHUNK), 1)
        == lax.rem(lax.broadcasted_iota(jnp.int32, (1, 8, CHUNK), 2), 8)
    ).astype(F32)

    def attention(at):
        cols = [[column(part, h) for part in range(3)] for h in range(HEADS)]
        q, k, v = (
            [qkv[at, cols[h][part]:cols[h][part] + HD] for h in range(HEADS)] for part in range(3)
        )
        da = [datt[at, h * HD:h * HD + HD] for h in range(HEADS)]
        scores = [dot(k[h], q[h], (1, 1)) for h in range(HEADS)]
        d_probs = [dot(v[h], da[h], (1, 1)) for h in range(HEADS)]
        probs_b, d_scores = [], []
        for h in range(HEADS):
            x = (scores[h] * inv).reshape(FRAMES, 8, CHUNK)
            e = jnp.exp(x - jnp.max(x, 0, keepdims=True))
            probs = e * (kept / jnp.sum(e, 0, keepdims=True))
            probs_b.append(probs.astype(BF16).reshape(CHUNK, CHUNK))
            dp_ = d_probs[h].reshape(FRAMES, 8, CHUNK)
            spread = jnp.sum(probs * dp_, 0, keepdims=True)
            d_scores.append((probs * (dp_ - spread) * inv).astype(BF16).reshape(CHUNK, CHUNK))
        attended = [dot(probs_b[h], v[h], (0, 0)).astype(BF16) for h in range(HEADS)]
        d_q = [dot(d_scores[h], k[h], (0, 0)).astype(BF16) for h in range(HEADS)]
        d_k = [dot(d_scores[h], q[h], (1, 0)).astype(BF16) for h in range(HEADS)]
        d_v = [dot(probs_b[h], da[h], (1, 0)).astype(BF16) for h in range(HEADS)]
        for h in range(HEADS):
            att[at, h * HD:h * HD + HD] = attended[h]
            for part, grad in enumerate((d_q, d_k, d_v)):
                dqkv[at, cols[h][part]:cols[h][part] + HD] = grad[h]

    def back_copy(part, d):
        to = pl.ds(pl.multiple_of(lax.rem(spot + d, 8) * 16, 16), 16)
        at = slice(2 * part, 2 * part + 2)
        return remote(
            d_in.at[at, to, :], back.at[part, d], b_send.at[part, d], b_recv.at[part, d], peer(d)
        )

    for part_ in range(2):
        two = slice(2 * part_, 2 * part_ + 2)
        at = slice(part_ * HALF_ROWS, part_ * HALF_ROWS + HALF_ROWS)
        for d in range(1, 8):
            spread_copy(0, part_, d).wait_recv()
        m = m_all[two].reshape(HALF_ROWS, WIDTH)
        qkv[at, :] = dot(m, wq_all[...], (1, 1)).astype(BF16)
        if part_ == 0:
            turned[:, at] = m.T
            turned_p[:, at] = dot(perm[...], m, (1, 1)).astype(BF16)
        for d in range(1, 8):
            spread_copy(1, part_, d).wait_recv()
        dbranch[at, :] = (gate * d_all[two].reshape(HALF_ROWS, WIDTH).astype(F32)).astype(BF16)
        datt[at, :] = dot(dbranch[at, :], wo_all[...], (1, 0)).astype(BF16)

        @pl.loop(2 * part_, 2 * part_ + 2)
        def _(c):
            attention(pl.ds(pl.multiple_of(c * CHUNK, CHUNK), CHUNK))

        for n in range(3):
            lanes = slice(n * 384, n * 384 + 384)
            grad = dot(dqkv[at, :], wq_all[:, lanes], (1, 0)).astype(BF16)
            d_in[two, :, lanes] = grad.reshape(2, CHUNK, 384)
        for d in range(1, 8):
            back_copy(part_, d).start()

    def block(size, z):
        return pl.ds(pl.multiple_of(z * size, 16), size)

    def pair_copy(i):
        at = block(BLOCK_Q, lax.rem(clip + OFFSETS[i], 8))
        return remote(gq.at[1 - core, at, :], xq.at[at, :], x_send.at[i], x_recv.at[i], twin)

    def pair_copy_o():
        return remote(go.at[1 - core], xo, y_send, y_recv, twin)

    slot = lax.broadcasted_iota(jnp.int32, (HEADS * SLOT_E, HEADS * HD), 0)
    inner = lax.rem(slot, SLOT_E)
    from_ = lax.div(inner, 9) * HD + lax.div(slot, SLOT_E) * 9 + lax.rem(inner, 9)
    pick = jnp.logical_and(
        lax.broadcasted_iota(jnp.int32, (HEADS * SLOT_E, HEADS * HD), 1) == from_, inner < HD
    )
    slots = dot(pick.astype(F32).astype(BF16), att[...], (1, 1)).astype(BF16)

    def out_terms(h):
        go[h] = dot(slots, dbranch[:, pl.ds(pl.multiple_of(h * START_O, 128), HALF_O)], (1, 0)).astype(BF16)

    def pair_copy_p():
        return remote(gp.at[1 - core], xp, yp_send, yp_recv, twin)

    def chain_terms(h):
        src = pl.ds(pl.multiple_of(h * HALF_Q, 128), CHAIN_LANES)
        gq[h] = dot(turned[...], dqkv[:, src], (1, 0)).astype(BF16)

    def plane_terms(h):
        src = pl.ds(pl.multiple_of(h * HALF_Q + CHAIN_LANES, 128), PLANE_LANES)
        gp[h] = dot(turned_p[...], dqkv[:, src], (1, 0)).astype(BF16)

    def plane_sends(copy, keep):
        for d in range(1, 8):
            for low in range(2):
                copy(d, low).start()
        for low in range(2):
            is_self = jnp.logical_and(core == half, core == low)

            @pl.when(is_self)
            def _():
                keep(low).start()

            @pl.when(jnp.logical_not(is_self))
            def _():
                copy(0, low).start()

    def plane_sent(copy):
        for d in range(1, 8):
            for low in range(2):
                copy(d, low).wait_send()
        for low in range(2):
            @pl.when(jnp.logical_or(core != half, core != low))
            def _():
                copy(0, low).wait_send()

    def plane_o(d, low):
        to = half * 8 + d
        return remote(
            stage_o.at[lax.rem(spot + d, 8), :, 256 * low:256 * low + 384], final_o.at[to],
            o_send.at[d, low], o_recv.at[to], owner(d, low),
        )

    def keep_o(low):
        return pltpu.make_async_copy(
            stage_o.at[spot, :, 256 * low:256 * low + 384], final_o.at[half * 8], o_recv.at[half * 8]
        )

    def plane_p(d):
        to = half * 8 + d
        return remote(
            stage_p.at[lax.rem(spot + d, 8)], final_p.at[to], op_send.at[d], op_recv.at[to], owner(d, 1)
        )

    late = m_all[2:4].reshape(HALF_ROWS, WIDTH)
    turned[:, HALF_ROWS:] = late.T
    chain_terms(1 - core)
    for i in range(8):
        pair_copy(i).start()
    chain_terms(core)

    def own(z, first, lanes):
        at = block(BLOCK_Q, z)
        return (
            gq[core, at, first:first + lanes].astype(F32) + xq[at, first:first + lanes].astype(F32)
        )

    def pieces(k, way):
        return FIRST_PIECES[way] if k == 0 else range(len(PIECES))

    def chain_copy(way, k, n):
        first, lanes = PIECES[n]
        return remote(
            sq.at[way, k, :, first:first + lanes], rq.at[way, k, :, first:first + lanes],
            c_send.at[way, k, n], c_recv.at[way, k, n], along(1 if way == 0 else 7),
        )

    def arrived(way, k, n):
        first, lanes = PIECES[n]
        chain_copy(way, k, n).wait_recv()
        return rq[way, k, :, first:first + lanes].astype(F32)

    def chain_step(k):
        for i in (0,) if k == 0 else (2 * k - 1, 2 * k):
            pair_copy(i).wait_recv()
        for n in range(len(PIECES)):
            for way in range(2):
                if n not in pieces(k, way):
                    continue
                first, lanes = PIECES[n]
                z = lax.rem(clip + (4 - k if way == 0 else 4 + k), 8)
                total = own(z, first, lanes)
                if k and n in pieces(k - 1, way):
                    total = total + arrived(way, k - 1, n)
                sq[way, k, :, first:first + lanes] = total.astype(BF16)
                chain_copy(way, k, n).start()

    chain_step(0)
    turned_p[:, HALF_ROWS:] = dot(perm[...], late, (1, 1)).astype(BF16)
    plane_terms(1 - core)
    pair_copy_p().start()
    out_terms(1 - core)
    pair_copy_o().start()
    plane_terms(core)
    out_terms(core)
    chain_step(1)
    pair_copy_o().wait_recv()
    for j in range(8):
        at = slice(SLOT_E * j, SLOT_E * j + SLOT_E)
        stage_o[j] = (go[core, at, :].astype(F32) + xo[at, :].astype(F32)).astype(BF16)
    plane_sends(plane_o, keep_o)

    pair_copy_p().wait_recv()
    for j in range(8):
        at = slice(BLOCK_Q * j, BLOCK_Q * j + BLOCK_Q)
        stage_p[j] = (gp[core, at, :].astype(F32) + xp[at, :].astype(F32)).astype(BF16)
    for d in range(1, 8):
        plane_p(d).start()
    own_p = jnp.logical_and(core == half, core == 1)

    @pl.when(own_p)
    def _():
        pltpu.make_async_copy(stage_p.at[spot], final_p.at[half * 8], op_recv.at[half * 8]).start()

    @pl.when(jnp.logical_not(own_p))
    def _():
        plane_p(0).start()

    gates = []
    for n in range(3):
        lanes = slice(n * 384, n * 384 + 384)
        branch = dot(att[...], wo_all[lanes, :], (1, 1))
        grads = d_all[:, :, lanes].reshape(ROWS, 384).astype(F32)
        gates.append(jnp.sum(branch * grads, 0, keepdims=True))
    gate_row = jnp.concatenate(gates, 1)

    def tokens_back(half_):
        def step(d, carry):
            b = back[half_, d].astype(F32).reshape(32, WIDTH)
            b = jnp.stack(
                [
                    jnp.concatenate([b[16 * g + 8 * f:16 * g + 8 * f + 8] for g in range(2)], 0)
                    for f in range(2)
                ],
                0,
            )
            at = patches(half_, lax.rem(spot + 8 - d, 8))
            normed, rstd = normalise(tok[:, at, :].astype(F32))
            d_normed = b * scale
            one = jnp.mean(d_normed, -1, keepdims=True)
            two = jnp.mean(d_normed * normed, -1, keepdims=True)
            out = dout[:, at, :].astype(F32) + rstd * (d_normed - one - normed * two)
            dout[:, at, :] = out.astype(BF16)
            return (
                carry[0] + jnp.sum(b.reshape(4, 8, WIDTH), 0),
                carry[1] + jnp.sum((b * normed).reshape(4, 8, WIDTH), 0),
            )

        return step

    chain_step(2)
    zero = jnp.zeros((8, WIDTH), F32)
    sums = (zero, zero)
    for part_ in range(2):
        back[part_, 0] = d_in[2 * part_:2 * part_ + 2, mine, :]
        for d in range(1, 8):
            back_copy(part_, d).wait_recv()
        sums = lax.fori_loop(0, 8, tokens_back(part_), sums, unroll=2)
        if part_ == 0:
            chain_step(3)
    result = pltpu.make_async_copy(dout, tok_out.at[0], here.at[4])
    result.start()
    flat = jnp.concatenate(
        [jnp.sum(sums[0], 0, keepdims=True), jnp.sum(sums[1], 0, keepdims=True), gate_row,
         jnp.zeros((1, 8 * PACKED - 3 * WIDTH), F32)], 1
    )
    part[...] = jnp.concatenate([flat[:, PACKED * i:PACKED * i + PACKED] for i in range(8)], 0)

    def part_copy(d):
        return remote(part, parts.at[d], p_send.at[d], p_recv.at[d], peer(d))

    for d in range(1, 8):
        part_copy(d).start()

    def widen(x, size, slot):
        count = 8 * slot
        row = lax.broadcasted_iota(jnp.int32, (count, x.shape[0]), 0)
        col = lax.broadcasted_iota(jnp.int32, (count, x.shape[0]), 1)
        inside = lax.rem(row, slot)
        pick = jnp.logical_and(col == lax.div(row, slot) * size + inside, inside < size)
        return dot(pick.astype(F32).astype(BF16), x, (1, 0)).astype(BF16)

    pair_copy(7).wait_recv()
    whole = []
    for n, (first, lanes) in enumerate(PIECES):
        total = own(clip, first, lanes)
        for way in range(2):
            total = total + arrived(way, 3, n)
        whole.append(total.astype(BF16))
    wide = widen(jnp.concatenate(whole, 1), 18, 32)
    stage[...] = wide.reshape(8, 32, CHAIN_LANES)

    def from_stage(j, low):
        return stage.at[j, :, 0:FINAL_LANES] if low == 0 else stage.at[j, :, 384:CHAIN_LANES]

    def to_final(i, low):
        return final.at[i] if low == 0 else final.at[i, :, 0:HIGH_LANES]

    def plane_q(d, low):
        to = half * 8 + d
        return remote(
            from_stage(lax.rem(spot + d, 8), low), to_final(to, low),
            f_send.at[d, low], f_recv.at[to], owner(d, low),
        )

    def keep_q(low):
        return pltpu.make_async_copy(from_stage(spot, low), to_final(half * 8, low), f_recv.at[half * 8])

    plane_sends(plane_q, keep_q)

    total = part[...]
    for d in range(1, 8):
        part_copy(d).wait_recv()
        total = total + parts[d]
    mods[clip] = total

    def mod_copy(d):
        ref = mods.at[clip]
        return remote(ref, ref, z_send.at[d], z_recv.at[d], along(d))

    for d in range(1, 8):
        mod_copy(d).start()

    def plane_sum(ref, sems):
        for i in range(16):
            wait_bytes(ref.at[i], sems.at[i])
        total = ref[0].astype(F32)
        for i in range(1, 16):
            total = total + ref[i].astype(F32)
        return total

    def last_copy(d):
        return remote(
            spread_o.at[lax.rem(clip + d, 8)], last_o.at[d], l_send.at[d], l_recv.at[d], along(d)
        )

    spread_o[...] = widen(plane_sum(final_o, o_recv).astype(BF16), 9, 16).reshape(8, 16, 384)
    for d in range(1, 8):
        last_copy(d).start()
    def last_copy_p(d):
        return remote(
            spread_p.at[lax.rem(clip + d, 8)], last_p.at[d], lp_send.at[d], lp_recv.at[d], along(d)
        )

    @pl.when(core == 1)
    def _():
        spread_p[...] = widen(plane_sum(final_p, op_recv).astype(BF16), 18, 32).reshape(8, 32, PLANE_LANES)
        for d in range(1, 8):
            last_copy_p(d).start()

    total = spread_o[clip].astype(F32)
    for d in range(1, 8):
        last_copy(d).wait_recv()
        total = total + last_o[d].astype(F32)
    first_o = 64 * half + 32 * core
    got_o = total[:, 0:SHARD_O]
    for start in (32, 64, 96):
        got_o = jnp.where(first_o == start, total[:, start:start + SHARD_O], got_o)
    oo[...] = got_o[0:9]
    for d in range(1, 8):
        mod_copy(d).wait()
    flats = [jnp.concatenate([mods[z, i:i + 1] for i in range(8)], 1) for z in range(8)]
    for i in range(3):
        d_mod[0, i] = jnp.concatenate([flat[:, WIDTH * i:WIDTH * i + WIDTH] for flat in flats], 0)
    @pl.when(core == 0)
    def _():
        oq[...] = plane_sum(final, f_recv)[0:18, 0:SHARD_Q]

    @pl.when(core == 1)
    def _():
        rest = spread_p[clip].astype(F32)
        for d in range(1, 8):
            last_copy_p(d).wait_recv()
            rest = rest + last_p[d].astype(F32)
        for i in range(16):
            wait_bytes(to_final(i, 1), f_recv.at[i])
        first = final[0, :, 0:HIGH_LANES].astype(F32)
        for i in range(1, 16):
            first = first + final[i, :, 0:HIGH_LANES].astype(F32)
        oq[...] = jnp.concatenate([first[0:18, 48:HIGH_LANES], rest[0:18, 0:SHARD_Q - HIGH_FIRST]], 1)
        for d in range(1, 8):
            last_copy_p(d).wait_send()

    for d in range(1, 8):
        plane_p(d).wait_send()

    @pl.when(jnp.logical_not(own_p))
    def _():
        plane_p(0).wait_send()

    pair_copy_p().wait_send()
    plane_sent(plane_o)
    plane_sent(plane_q)
    for d in range(1, 8):
        last_copy(d).wait_send()
        part_copy(d).wait_send()
        for part_ in range(2):
            back_copy(part_, d).wait_send()
            for i in range(2):
                spread_copy(i, part_, d).wait_send()
    pair_copy_o().wait_send()
    for n in range(2):
        own_copy(n).wait_send()
    for i in range(8):
        pair_copy(i).wait_send()
    for k in range(STEPS):
        for way in range(2):
            for n in pieces(k, way):
                chain_copy(way, k, n).wait_send()

    def sent(parity):
        for i in range(4):
            for n in range(2):
                across_copy(n, parity, i).wait_send()
                along_copy(n, parity, i).wait_send()
                twin_copy(n, parity, i, 0).wait_send()
                twin_copy(n, 1 - parity, i, 1).wait_send()

    by_parity(clip, sent)
    result.wait()


def copy_kernel(*refs):
    count = (len(refs) - 1) // 2
    copies = [
        pltpu.make_async_copy(refs[i], refs[count + i], refs[-1].at[i]) for i in range(count)
    ]
    for copy in copies:
        copy.start()
    for copy in copies:
        copy.wait()


def body(tokens, d_out, modulation, w_qkv, w_out):
    dma = pltpu.SemaphoreType.DMA

    def held(*shape, dtype=BF16):
        return pltpu.VMEM(shape, dtype)

    anywhere = pl.BlockSpec(memory_space=pl.ANY)
    inside = pl.BlockSpec(memory_space=pltpu.VMEM)
    outs = [
        jax.ShapeDtypeStruct(tokens.shape, BF16),
        jax.ShapeDtypeStruct((1, 3, 8, WIDTH), F32),
        jax.ShapeDtypeStruct((18, SHARD_Q), F32),
        jax.ShapeDtypeStruct((9, SHARD_O), F32),
    ]
    chains = (2, STEPS, len(PIECES))
    results = pl.pallas_call(
        fused_kernel,
        out_shape=outs,
        in_specs=[anywhere, anywhere, inside, anywhere, anywhere],
        out_specs=[anywhere, inside, inside, inside],
        scratch_shapes=[
            held(2, 256, WIDTH), held(2, 256, WIDTH),
            held(2, 8, 2, 16, WIDTH), held(2, 8, 2, 16, WIDTH),
            held(CHUNKS, CHUNK, WIDTH), held(CHUNKS, CHUNK, WIDTH),
            held(2 * HALF_Q, WIDTH), held(WIDTH, HEADS * HD),
            held(ROWS, 2 * HALF_Q), held(ROWS, HEADS * HD), held(ROWS, HEADS * HD),
            held(ROWS, WIDTH), held(ROWS, 2 * HALF_Q),
            held(WIDTH, ROWS), held(WIDTH, ROWS), held(WIDTH, WIDTH), held(CHUNKS, CHUNK, WIDTH),
            held(2, WIDTH, CHAIN_LANES), held(2, WIDTH, PLANE_LANES), held(2, HEADS * SLOT_E, HALF_O),
            held(2, 8, 2, 16, WIDTH),
            held(WIDTH, CHAIN_LANES), held(WIDTH, PLANE_LANES), held(HEADS * SLOT_E, HALF_O),
            held(2, STEPS, BLOCK_Q, CHAIN_LANES), held(2, STEPS, BLOCK_Q, CHAIN_LANES),
            held(8, 32, CHAIN_LANES), held(16, 32, FINAL_LANES),
            held(8, BLOCK_Q, PLANE_LANES), held(16, BLOCK_Q, PLANE_LANES),
            held(8, 32, PLANE_LANES), held(8, 32, PLANE_LANES),
            held(8, SLOT_E, HALF_O), held(16, SLOT_E, 384),
            held(8, 16, 384), held(8, 16, 384),
            held(8, PACKED, dtype=F32), held(8, 8, PACKED, dtype=F32), held(8, 8, PACKED, dtype=F32),
            dma((5,)), dma((2, 2, 8)), dma((2, 2, 8)), dma((2,)), dma((2,)),
            dma((2, 4)), dma((2, 4)), dma((2, 4)), dma((2, 4)), dma((2, 4, 2)), dma((2, 4, 2)),
            dma((2, 8)), dma((2, 8)), dma((8,)), dma((8,)), dma(chains), dma(chains),
            dma((8,)), dma((8,)), dma((8,)), dma((8,)), dma((8, 2)), dma((16,)),
            dma, dma, dma((8, 2)), dma((16,)), dma((8,)), dma((8,)),
            dma, dma, dma((8,)), dma((16,)), dma((8,)), dma((8,)),
        ],
        compiler_params=pltpu.CompilerParams(
            vmem_limit_bytes=VMEM_BYTES, collective_id=0, has_side_effects=True
        ),
    )(tokens, d_out, jnp.swapaxes(modulation, 1, 2), w_qkv, w_out)
    d_tokens, d_mod, g_qkv, g_out = pl.pallas_call(
        copy_kernel,
        out_shape=outs,
        in_specs=[anywhere] * 4,
        out_specs=[inside] * 4,
        scratch_shapes=[dma((4,))],
        compiler_params=pltpu.CompilerParams(vmem_limit_bytes=VMEM_BYTES),
    )(*results)
    return d_tokens, jnp.swapaxes(d_mod, 1, 2), g_qkv.T, g_out.T


def solution(mesh):
    in_specs = (
        P("dp", "seq", None, None),
        P("dp", "seq", None, None),
        P("dp", None, None, None),
        P("dp", None),
        P("dp", None),
    )
    out_specs = (
        P("dp", "seq", None, None),
        P("dp", None, None, None),
        P("dp", "seq"),
        P("dp", "seq"),
    )
    return jax.shard_map(body, mesh=mesh, in_specs=in_specs, out_specs=out_specs, check_vma=False)
```

```python
import math

import jax
import jax.numpy as jnp
from jax import lax
from jax.experimental import pallas as pl
from jax.experimental.pallas import tpu as pltpu
from jax.sharding import PartitionSpec as P

MESH = pl.DeviceIdType.MESH
F32 = jnp.float32
BF16 = jnp.bfloat16

WIDTH = 1152
HEADS = 8
HD = 72
FRAMES = 16
CLIP_DEVICES = 8
CHUNKS = 4
CHUNK = 128
ROWS = 512
SHARD_Q = 432
SHARD_O = 288
HALF_Q = 896
HALF_O = 640
START_O = 512
SLOT_E = 80
EPS = 1e-06
VMEM_BYTES = 56 * 1024 * 1024

PIECES = ((0, 256), (256, 256), (512, 384))
FIRST_PIECES = ((0, 1), (2,))
CHAIN_LANES = 896
FINAL_LANES = 512
BLOCK_Q = 144
PACKED = 512

OFFSETS = (4, 3, 5, 2, 6, 1, 7, 0)
STEPS = 4
HALF_ROWS = 256

PIECES_WQ = (((0, 64), (64, 48), (112, 64), (176, 48)), ((224, 64), (288, 48), (336, 48), (384, 48)))
PIECES_WO = (((0, 48), (48, 32), (80, 32), (112, 32)), ((144, 48), (192, 32), (224, 32), (256, 32)))


def dot(left, right, contract):
    return lax.dot_general(
        left, right, ((contract[:1], contract[1:]), ((), ())), preferred_element_type=F32
    )


def place():
    seq, dp = lax.axis_index("seq"), lax.axis_index("dp")
    clip, spot = lax.div(seq, 8), lax.rem(seq, 8)
    half, core = lax.div(dp, 2), lax.rem(dp, 2)
    return seq, dp, clip, spot, half, core


def column(part, head):
    block = part * HEADS + head
    return block * HD if block < 12 else HALF_Q + (block - 12) * HD


def normalise(x):
    center = x - jnp.mean(x, -1, keepdims=True)
    var = jnp.mean(center * center, -1, keepdims=True)
    rstd = lax.rsqrt(var + EPS)
    return center * rstd, rstd


def signal_all(barrier, devices):
    for device in devices:
        pl.semaphore_signal(barrier, inc=1, device_id=device, device_id_type=MESH)


def by_parity(clip, act):
    for parity in range(2):
        @pl.when(lax.rem(clip, 2) == parity)
        def _():
            act(parity)


def wait_bytes(ref, sem):
    pltpu.make_async_copy(ref, ref, sem).wait()


def fused_kernel(
    tok_in, dout_in, mod, wq, wo, tok_out, d_mod, oq, oo,
    tok, dout, m_send, d_send, m_all, d_all, wq_all, wo_all,
    qkv, datt, att, dbranch, dqkv, turned, d_in, gq, go,
    back, xq, xo, sq, rq, stage, final, stage_o, final_o, spread_o, last_o, part, parts, mods,
    here, a_send, a_recv, own_send, own_recv, w_send, w_recv, v_send, v_recv, t_send, t_recv,
    b_send, b_recv, x_send, x_recv, c_send, c_recv, p_send, p_recv,
    z_send, z_recv, f_send, f_recv, y_send, y_recv, o_send, o_recv, l_send, l_recv,
):
    seq, dp, clip, spot, half, core = place()
    twin = {"seq": seq, "dp": half * 2 + 1 - core}
    across = {
        "seq": clip * 8 + (1 - lax.div(spot, 4)) * 4 + lax.rem(spot, 4),
        "dp": (1 - half) * 2 + core,
    }

    def peer(d):
        return {"seq": clip * 8 + lax.rem(spot + d, 8), "dp": dp}

    def along(d):
        return {"seq": lax.rem(clip + d, 8) * 8 + spot, "dp": dp}

    def owner(d, low):
        return {"seq": clip * 8 + lax.rem(spot + d, 8), "dp": core * 2 + low}

    def source(d, h):
        return {"seq": clip * 8 + lax.rem(spot + 8 - d, 8), "dp": h * 2 + half}

    def remote(src, dst, send, recv, device):
        return pltpu.make_async_remote_copy(
            src_ref=src, dst_ref=dst, send_sem=send, recv_sem=recv,
            device_id=device, device_id_type=MESH,
        )

    loads = [
        pltpu.make_async_copy(tok_in.at[0], tok, here.at[0]),
        pltpu.make_async_copy(dout_in.at[0], dout, here.at[1]),
    ]
    for copy in loads:
        copy.start()
    barrier = pltpu.get_barrier_semaphore()
    signal_all(barrier, [twin, across] + [peer(d) for d in range(1, 8)] + [along(d) for d in range(1, 8)])
    signal_all(barrier, [source(d, h) for d in range(1, 8) for h in range(2)])
    for h in range(2):
        @pl.when(jnp.logical_or(half != core, h != half))
        def _():
            signal_all(barrier, [source(0, h)])

    shards, wholes = (wq, wo), (wq_all, wo_all)

    def first_row(n, h, c):
        return h * HALF_Q + c * SHARD_Q if n == 0 else (h * 2 + c) * SHARD_O

    def rows(n, h, c, at):
        return wholes[n].at[pl.ds(pl.multiple_of(first_row(n, h, c) + at[0], 16), at[1])]

    def entire(n):
        return (0, (SHARD_Q, SHARD_O)[n])

    def piece(n, parity, i):
        return (PIECES_WQ, PIECES_WO)[n][parity][i]

    def own_copy(n):
        return remote(shards[n], rows(n, half, core, entire(n)), own_send.at[n], own_recv.at[n], twin)

    def keep_copy(n):
        return pltpu.make_async_copy(shards[n], rows(n, half, core, entire(n)), here.at[2 + n])

    def across_copy(n, parity, i):
        at = piece(n, parity, i)
        return remote(
            shards[n].at[pl.ds(at[0], at[1])], rows(n, half, core, at),
            w_send.at[n, i], w_recv.at[n, i], across,
        )

    def passed(n, parity, i):
        return rows(n, 1 - half, core, piece(n, parity, i))

    def along_copy(n, parity, i):
        ref = passed(n, parity, i)
        return remote(ref, ref, v_send.at[n, i], v_recv.at[n, i], along(1 if i % 2 == 0 else 7))

    def twin_copy(n, parity, i, own):
        ref = passed(n, parity, i)
        return remote(ref, ref, t_send.at[n, i, own], t_recv.at[n, i, own], twin)

    def send_across(parity):
        for i in range(4):
            for n in range(2):
                across_copy(n, parity, i).start()

    zeros = jnp.zeros((HALF_Q - 2 * SHARD_Q, WIDTH), BF16)
    wq_all[2 * SHARD_Q:HALF_Q, :] = zeros
    wq_all[HALF_Q + 2 * SHARD_Q:, :] = zeros

    own_mod = mod[0, :, pl.ds(clip, 1), :].reshape(3, WIDTH)
    shift, scale, gate = own_mod[0:1], 1.0 + own_mod[1:2], own_mod[2:3]
    mine = pl.ds(pl.multiple_of(spot * 16, 16), 16)

    def arranged(x):
        return jnp.concatenate(
            [x[f, 8 * g:8 * g + 8] for g in range(2) for f in range(2)], 0
        ).astype(BF16).reshape(2, 16, WIDTH)

    def patches(part, j):
        return pl.ds(pl.multiple_of(j * 32 + part * 16, 16), 16)

    def blocks(part, d):
        at = patches(part, lax.rem(spot + d, 8))
        normed, _ = normalise(tok[:, at, :].astype(F32))
        return arranged(normed * scale + shift), arranged(dout[:, at, :].astype(F32))

    def spread_copy(i, part, d):
        src, dst = ((m_send, m_all), (d_send, d_all))[i]
        return remote(
            src.at[part, d], dst.at[2 * part:2 * part + 2, mine, :],
            a_send.at[i, part, d], a_recv.at[i, part, d], peer(d),
        )

    def spread(i, part):
        @pl.loop(1, 8)
        def _(d):
            spread_copy(i, part, d).start()

    for n in range(2):
        keep_copy(n).start()
    for copy in loads:
        copy.wait()

    def prepare(part, d):
        m_send[part, d], d_send[part, d] = blocks(part, d)

    def prepare_step(part):
        def step(d, carry):
            prepare(part, d)
            return carry

        return step

    lax.fori_loop(0, 8, prepare_step(0), 0, unroll=2)
    pl.semaphore_wait(barrier, jnp.where(half == core, 31, 32))
    by_parity(clip, send_across)

    spread(0, 0)
    spread(1, 0)
    for n in range(2):
        own_copy(n).start()

    @pl.loop(1, 8)
    def _(d):
        prepare(1, d)
        spread_copy(0, 1, d).start()

    prepare(1, 0)
    for part_ in range(2):
        at = slice(2 * part_, 2 * part_ + 2)
        m_all[at, mine, :], d_all[at, mine, :] = m_send[part_, 0], d_send[part_, 0]

    for start in (2 * SHARD_Q, HALF_Q + 2 * SHARD_Q):
        dqkv[:, start:start + 32] = jnp.zeros((ROWS, 32), BF16)

    for i in range(4):
        def hand_on(parity):
            for n in range(2):
                across_copy(n, parity, i).wait_recv()
                along_copy(n, parity, i).start()
                twin_copy(n, parity, i, 0).start()

        by_parity(clip, hand_on)
        if i == 1:
            spread(1, 1)
    for i in range(4):
        def hand_twin(parity):
            for n in range(2):
                along_copy(n, 1 - parity, i).wait_recv()
                twin_copy(n, 1 - parity, i, 1).start()

        by_parity(clip, hand_twin)
    for n in range(2):
        keep_copy(n).wait()
        own_copy(n).wait_recv()

    def from_twin(parity):
        for i in range(4):
            for n in range(2):
                twin_copy(n, parity, i, 0).wait_recv()
                twin_copy(n, 1 - parity, i, 1).wait_recv()

    by_parity(clip, from_twin)

    inv = 1.0 / math.sqrt(HD)
    kept = (
        lax.broadcasted_iota(jnp.int32, (1, 8, CHUNK), 1)
        == lax.rem(lax.broadcasted_iota(jnp.int32, (1, 8, CHUNK), 2), 8)
    ).astype(F32)

    def attention(at):
        cols = [[column(part, h) for part in range(3)] for h in range(HEADS)]
        q, k, v = (
            [qkv[at, cols[h][part]:cols[h][part] + HD] for h in range(HEADS)] for part in range(3)
        )
        da = [datt[at, h * HD:h * HD + HD] for h in range(HEADS)]
        scores = [dot(k[h], q[h], (1, 1)) for h in range(HEADS)]
        d_probs = [dot(v[h], da[h], (1, 1)) for h in range(HEADS)]
        probs_b, d_scores = [], []
        for h in range(HEADS):
            x = (scores[h] * inv).reshape(FRAMES, 8, CHUNK)
            e = jnp.exp(x - jnp.max(x, 0, keepdims=True))
            probs = e * (kept / jnp.sum(e, 0, keepdims=True))
            probs_b.append(probs.astype(BF16).reshape(CHUNK, CHUNK))
            dp_ = d_probs[h].reshape(FRAMES, 8, CHUNK)
            spread = jnp.sum(probs * dp_, 0, keepdims=True)
            d_scores.append((probs * (dp_ - spread) * inv).astype(BF16).reshape(CHUNK, CHUNK))
        attended = [dot(probs_b[h], v[h], (0, 0)).astype(BF16) for h in range(HEADS)]
        d_q = [dot(d_scores[h], k[h], (0, 0)).astype(BF16) for h in range(HEADS)]
        d_k = [dot(d_scores[h], q[h], (1, 0)).astype(BF16) for h in range(HEADS)]
        d_v = [dot(probs_b[h], da[h], (1, 0)).astype(BF16) for h in range(HEADS)]
        for h in range(HEADS):
            att[at, h * HD:h * HD + HD] = attended[h]
            for part, grad in enumerate((d_q, d_k, d_v)):
                dqkv[at, cols[h][part]:cols[h][part] + HD] = grad[h]

    def back_copy(part, d):
        to = pl.ds(pl.multiple_of(lax.rem(spot + d, 8) * 16, 16), 16)
        at = slice(2 * part, 2 * part + 2)
        return remote(
            d_in.at[at, to, :], back.at[part, d], b_send.at[part, d], b_recv.at[part, d], peer(d)
        )

    for part_ in range(2):
        two = slice(2 * part_, 2 * part_ + 2)
        at = slice(part_ * HALF_ROWS, part_ * HALF_ROWS + HALF_ROWS)
        for d in range(1, 8):
            spread_copy(0, part_, d).wait_recv()
        m = m_all[two].reshape(HALF_ROWS, WIDTH)
        qkv[at, :] = dot(m, wq_all[...], (1, 1)).astype(BF16)
        if part_ == 0:
            turned[:, at] = m.T
        for d in range(1, 8):
            spread_copy(1, part_, d).wait_recv()
        dbranch[at, :] = (gate * d_all[two].reshape(HALF_ROWS, WIDTH).astype(F32)).astype(BF16)
        datt[at, :] = dot(dbranch[at, :], wo_all[...], (1, 0)).astype(BF16)

        @pl.loop(2 * part_, 2 * part_ + 2)
        def _(c):
            attention(pl.ds(pl.multiple_of(c * CHUNK, CHUNK), CHUNK))

        for n in range(3):
            lanes = slice(n * 384, n * 384 + 384)
            grad = dot(dqkv[at, :], wq_all[:, lanes], (1, 0)).astype(BF16)
            d_in[two, :, lanes] = grad.reshape(2, CHUNK, 384)
        for d in range(1, 8):
            back_copy(part_, d).start()

    def block(size, z):
        return pl.ds(pl.multiple_of(z * size, 16), size)

    def pair_copy(i):
        at = block(BLOCK_Q, lax.rem(clip + OFFSETS[i], 8))
        return remote(gq.at[1 - core, at, :], xq.at[at, :], x_send.at[i], x_recv.at[i], twin)

    def pair_copy_o():
        return remote(go.at[1 - core], xo, y_send, y_recv, twin)

    slot = lax.broadcasted_iota(jnp.int32, (HEADS * SLOT_E, HEADS * HD), 0)
    inner = lax.rem(slot, SLOT_E)
    from_ = lax.div(inner, 9) * HD + lax.div(slot, SLOT_E) * 9 + lax.rem(inner, 9)
    pick = jnp.logical_and(
        lax.broadcasted_iota(jnp.int32, (HEADS * SLOT_E, HEADS * HD), 1) == from_, inner < HD
    )
    slots = dot(pick.astype(F32).astype(BF16), att[...], (1, 1)).astype(BF16)

    def out_terms(h):
        go[h] = dot(slots, dbranch[:, pl.ds(pl.multiple_of(h * START_O, 128), HALF_O)], (1, 0)).astype(BF16)

    def chain_terms(h):
        src = pl.ds(pl.multiple_of(h * HALF_Q, 128), CHAIN_LANES)
        gq[h] = dot(turned[...], dqkv[:, src], (1, 0)).astype(BF16)

    def plane_sends(copy, keep):
        for d in range(1, 8):
            for low in range(2):
                copy(d, low).start()
        for low in range(2):
            is_self = jnp.logical_and(core == half, core == low)

            @pl.when(is_self)
            def _():
                keep(low).start()

            @pl.when(jnp.logical_not(is_self))
            def _():
                copy(0, low).start()

    def plane_sent(copy):
        for d in range(1, 8):
            for low in range(2):
                copy(d, low).wait_send()
        for low in range(2):
            @pl.when(jnp.logical_or(core != half, core != low))
            def _():
                copy(0, low).wait_send()

    def plane_o(d, low):
        to = half * 8 + d
        return remote(
            stage_o.at[lax.rem(spot + d, 8), :, 256 * low:256 * low + 384], final_o.at[to],
            o_send.at[d, low], o_recv.at[to], owner(d, low),
        )

    def keep_o(low):
        return pltpu.make_async_copy(
            stage_o.at[spot, :, 256 * low:256 * low + 384], final_o.at[half * 8], o_recv.at[half * 8]
        )

    late = m_all[2:4].reshape(HALF_ROWS, WIDTH)
    turned[:, HALF_ROWS:] = late.T
    chain_terms(1 - core)
    for i in range(8):
        pair_copy(i).start()
    chain_terms(core)

    def own(z, first, lanes):
        at = block(BLOCK_Q, z)
        return (
            gq[core, at, first:first + lanes].astype(F32) + xq[at, first:first + lanes].astype(F32)
        )

    def pieces(k, way):
        return FIRST_PIECES[way] if k == 0 else range(len(PIECES))

    def chain_copy(way, k, n):
        first, lanes = PIECES[n]
        return remote(
            sq.at[way, k, :, first:first + lanes], rq.at[way, k, :, first:first + lanes],
            c_send.at[way, k, n], c_recv.at[way, k, n], along(1 if way == 0 else 7),
        )

    def arrived(way, k, n):
        first, lanes = PIECES[n]
        chain_copy(way, k, n).wait_recv()
        return rq[way, k, :, first:first + lanes].astype(F32)

    def chain_step(k):
        for i in (0,) if k == 0 else (2 * k - 1, 2 * k):
            pair_copy(i).wait_recv()
        for n in range(len(PIECES)):
            for way in range(2):
                if n not in pieces(k, way):
                    continue
                first, lanes = PIECES[n]
                z = lax.rem(clip + (4 - k if way == 0 else 4 + k), 8)
                total = own(z, first, lanes)
                if k and n in pieces(k - 1, way):
                    total = total + arrived(way, k - 1, n)
                sq[way, k, :, first:first + lanes] = total.astype(BF16)
                chain_copy(way, k, n).start()

    chain_step(0)
    out_terms(1 - core)
    pair_copy_o().start()
    out_terms(core)
    chain_step(1)
    pair_copy_o().wait_recv()
    for j in range(8):
        at = slice(SLOT_E * j, SLOT_E * j + SLOT_E)
        stage_o[j] = (go[core, at, :].astype(F32) + xo[at, :].astype(F32)).astype(BF16)
    plane_sends(plane_o, keep_o)

    gates = []
    for n in range(3):
        lanes = slice(n * 384, n * 384 + 384)
        branch = dot(att[...], wo_all[lanes, :], (1, 1))
        grads = d_all[:, :, lanes].reshape(ROWS, 384).astype(F32)
        gates.append(jnp.sum(branch * grads, 0, keepdims=True))
    gate_row = jnp.concatenate(gates, 1)

    def tokens_back(half_):
        def step(d, carry):
            b = back[half_, d].astype(F32).reshape(32, WIDTH)
            b = jnp.stack(
                [
                    jnp.concatenate([b[16 * g + 8 * f:16 * g + 8 * f + 8] for g in range(2)], 0)
                    for f in range(2)
                ],
                0,
            )
            at = patches(half_, lax.rem(spot + 8 - d, 8))
            normed, rstd = normalise(tok[:, at, :].astype(F32))
            d_normed = b * scale
            one = jnp.mean(d_normed, -1, keepdims=True)
            two = jnp.mean(d_normed * normed, -1, keepdims=True)
            out = dout[:, at, :].astype(F32) + rstd * (d_normed - one - normed * two)
            dout[:, at, :] = out.astype(BF16)
            return (
                carry[0] + jnp.sum(b.reshape(4, 8, WIDTH), 0),
                carry[1] + jnp.sum((b * normed).reshape(4, 8, WIDTH), 0),
            )

        return step

    chain_step(2)
    zero = jnp.zeros((8, WIDTH), F32)
    sums = (zero, zero)
    for part_ in range(2):
        back[part_, 0] = d_in[2 * part_:2 * part_ + 2, mine, :]
        for d in range(1, 8):
            back_copy(part_, d).wait_recv()
        sums = lax.fori_loop(0, 8, tokens_back(part_), sums, unroll=2)
        if part_ == 0:
            chain_step(3)
    result = pltpu.make_async_copy(dout, tok_out.at[0], here.at[4])
    result.start()
    flat = jnp.concatenate(
        [jnp.sum(sums[0], 0, keepdims=True), jnp.sum(sums[1], 0, keepdims=True), gate_row,
         jnp.zeros((1, 8 * PACKED - 3 * WIDTH), F32)], 1
    )
    part[...] = jnp.concatenate([flat[:, PACKED * i:PACKED * i + PACKED] for i in range(8)], 0)

    def part_copy(d):
        return remote(part, parts.at[d], p_send.at[d], p_recv.at[d], peer(d))

    for d in range(1, 8):
        part_copy(d).start()

    def widen(x, size, slot):
        count = 8 * slot
        row = lax.broadcasted_iota(jnp.int32, (count, x.shape[0]), 0)
        col = lax.broadcasted_iota(jnp.int32, (count, x.shape[0]), 1)
        inside = lax.rem(row, slot)
        pick = jnp.logical_and(col == lax.div(row, slot) * size + inside, inside < size)
        return dot(pick.astype(F32).astype(BF16), x, (1, 0)).astype(BF16)

    pair_copy(7).wait_recv()
    whole = []
    for n, (first, lanes) in enumerate(PIECES):
        total = own(clip, first, lanes)
        for way in range(2):
            total = total + arrived(way, 3, n)
        whole.append(total.astype(BF16))
    wide = widen(jnp.concatenate(whole, 1), 18, 32)
    stage[...] = wide.reshape(8, 32, CHAIN_LANES)

    def from_stage(j, low):
        return stage.at[j, :, 384 * low:384 * low + FINAL_LANES]

    def plane_q(d, low):
        to = half * 8 + d
        return remote(
            from_stage(lax.rem(spot + d, 8), low), final.at[to],
            f_send.at[d, low], f_recv.at[to], owner(d, low),
        )

    def keep_q(low):
        return pltpu.make_async_copy(from_stage(spot, low), final.at[half * 8], f_recv.at[half * 8])

    plane_sends(plane_q, keep_q)

    total = part[...]
    for d in range(1, 8):
        part_copy(d).wait_recv()
        total = total + parts[d]
    mods[clip] = total

    def mod_copy(d):
        ref = mods.at[clip]
        return remote(ref, ref, z_send.at[d], z_recv.at[d], along(d))

    for d in range(1, 8):
        mod_copy(d).start()

    def plane_sum(ref, sems):
        for i in range(16):
            wait_bytes(ref.at[i], sems.at[i])
        total = ref[0].astype(F32)
        for i in range(1, 16):
            total = total + ref[i].astype(F32)
        return total

    def last_copy(d):
        return remote(
            spread_o.at[lax.rem(clip + d, 8)], last_o.at[d], l_send.at[d], l_recv.at[d], along(d)
        )

    spread_o[...] = widen(plane_sum(final_o, o_recv).astype(BF16), 9, 16).reshape(8, 16, 384)
    for d in range(1, 8):
        last_copy(d).start()
    total = spread_o[clip].astype(F32)
    for d in range(1, 8):
        last_copy(d).wait_recv()
        total = total + last_o[d].astype(F32)
    first_o = 64 * half + 32 * core
    got_o = total[:, 0:SHARD_O]
    for start in (32, 64, 96):
        got_o = jnp.where(first_o == start, total[:, start:start + SHARD_O], got_o)
    oo[...] = got_o[0:9]
    for d in range(1, 8):
        mod_copy(d).wait()
    flats = [jnp.concatenate([mods[z, i:i + 1] for i in range(8)], 1) for z in range(8)]
    for i in range(3):
        d_mod[0, i] = jnp.concatenate([flat[:, WIDTH * i:WIDTH * i + WIDTH] for flat in flats], 0)
    total = plane_sum(final, f_recv)
    oq[...] = jnp.where(core == 0, total[:, 0:SHARD_Q], total[:, 48:48 + SHARD_Q])[0:18]

    plane_sent(plane_o)
    plane_sent(plane_q)
    for d in range(1, 8):
        last_copy(d).wait_send()
        part_copy(d).wait_send()
        for part_ in range(2):
            back_copy(part_, d).wait_send()
            for i in range(2):
                spread_copy(i, part_, d).wait_send()
    pair_copy_o().wait_send()
    for n in range(2):
        own_copy(n).wait_send()
    for i in range(8):
        pair_copy(i).wait_send()
    for k in range(STEPS):
        for way in range(2):
            for n in pieces(k, way):
                chain_copy(way, k, n).wait_send()

    def sent(parity):
        for i in range(4):
            for n in range(2):
                across_copy(n, parity, i).wait_send()
                along_copy(n, parity, i).wait_send()
                twin_copy(n, parity, i, 0).wait_send()
                twin_copy(n, 1 - parity, i, 1).wait_send()

    by_parity(clip, sent)
    result.wait()


def copy_kernel(*refs):
    count = (len(refs) - 1) // 2
    copies = [
        pltpu.make_async_copy(refs[i], refs[count + i], refs[-1].at[i]) for i in range(count)
    ]
    for copy in copies:
        copy.start()
    for copy in copies:
        copy.wait()


def body(tokens, d_out, modulation, w_qkv, w_out):
    dma = pltpu.SemaphoreType.DMA

    def held(*shape, dtype=BF16):
        return pltpu.VMEM(shape, dtype)

    anywhere = pl.BlockSpec(memory_space=pl.ANY)
    inside = pl.BlockSpec(memory_space=pltpu.VMEM)
    outs = [
        jax.ShapeDtypeStruct(tokens.shape, BF16),
        jax.ShapeDtypeStruct((1, 3, 8, WIDTH), F32),
        jax.ShapeDtypeStruct((18, SHARD_Q), F32),
        jax.ShapeDtypeStruct((9, SHARD_O), F32),
    ]
    chains = (2, STEPS, len(PIECES))
    results = pl.pallas_call(
        fused_kernel,
        out_shape=outs,
        in_specs=[anywhere, anywhere, inside, anywhere, anywhere],
        out_specs=[anywhere, inside, inside, inside],
        scratch_shapes=[
            held(2, 256, WIDTH), held(2, 256, WIDTH),
            held(2, 8, 2, 16, WIDTH), held(2, 8, 2, 16, WIDTH),
            held(CHUNKS, CHUNK, WIDTH), held(CHUNKS, CHUNK, WIDTH),
            held(2 * HALF_Q, WIDTH), held(WIDTH, HEADS * HD),
            held(ROWS, 2 * HALF_Q), held(ROWS, HEADS * HD), held(ROWS, HEADS * HD),
            held(ROWS, WIDTH), held(ROWS, 2 * HALF_Q),
            held(WIDTH, ROWS), held(CHUNKS, CHUNK, WIDTH),
            held(2, WIDTH, CHAIN_LANES), held(2, HEADS * SLOT_E, HALF_O),
            held(2, 8, 2, 16, WIDTH),
            held(WIDTH, CHAIN_LANES), held(HEADS * SLOT_E, HALF_O),
            held(2, STEPS, BLOCK_Q, CHAIN_LANES), held(2, STEPS, BLOCK_Q, CHAIN_LANES),
            held(8, 32, CHAIN_LANES), held(16, 32, FINAL_LANES),
                       held(8, SLOT_E, HALF_O), held(16, SLOT_E, 384),
            held(8, 16, 384), held(8, 16, 384),
            held(8, PACKED, dtype=F32), held(8, 8, PACKED, dtype=F32), held(8, 8, PACKED, dtype=F32),
            dma((5,)), dma((2, 2, 8)), dma((2, 2, 8)), dma((2,)), dma((2,)),
            dma((2, 4)), dma((2, 4)), dma((2, 4)), dma((2, 4)), dma((2, 4, 2)), dma((2, 4, 2)),
            dma((2, 8)), dma((2, 8)), dma((8,)), dma((8,)), dma(chains), dma(chains),
            dma((8,)), dma((8,)), dma((8,)), dma((8,)), dma((8, 2)), dma((16,)),
            dma, dma, dma((8, 2)), dma((16,)), dma((8,)), dma((8,)),
        ],
        compiler_params=pltpu.CompilerParams(
            vmem_limit_bytes=VMEM_BYTES, collective_id=0, has_side_effects=True
        ),
    )(tokens, d_out, jnp.swapaxes(modulation, 1, 2), w_qkv, w_out)
    d_tokens, d_mod, g_qkv, g_out = pl.pallas_call(
        copy_kernel,
        out_shape=outs,
        in_specs=[anywhere] * 4,
        out_specs=[inside] * 4,
        scratch_shapes=[dma((4,))],
        compiler_params=pltpu.CompilerParams(vmem_limit_bytes=VMEM_BYTES),
    )(*results)
    return d_tokens, jnp.swapaxes(d_mod, 1, 2), g_qkv.T, g_out.T


def solution(mesh):
    in_specs = (
        P("dp", "seq", None, None),
        P("dp", "seq", None, None),
        P("dp", None, None, None),
        P("dp", None),
        P("dp", None),
    )
    out_specs = (
        P("dp", "seq", None, None),
        P("dp", None, None, None),
        P("dp", "seq"),
        P("dp", "seq"),
    )
    return jax.shard_map(body, mesh=mesh, in_specs=in_specs, out_specs=out_specs, check_vma=False)
```
